32 devices in a mesh: dp: 16 (over z, y, core), centre: 2 (over x).
Axes of the slice: x: 2, y: 2, z: 4, core: 2. Of those that a mesh axis runs over, the one named last changes fastest.
Arguments:
- samples: float32 [8192, 512], P('dp'), may hold values from -4 to 4
- targets: float32 [8192, 64], P('dp'), may hold values from -6 to 6
- centres: float32 [4096, 512], P('centre'), may hold values from -4 to 4
- coefficients: float32 [4096, 64], P('centre'), may hold values from -0.9 to 0.9
Outputs:
- residual: float32 [8192, 64], P('dp')
- new_coefficients: float32 [4096, 64], P(('centre', 'dp'))
The draws below stay inside these ranges and needn't reach their ends.
All inputs are finite; a program needn't handle non-finite values.
Results may differ from the reference program's by a relative error of at most 0.0001.
Values sent between devices are 32-bit elements; how exact they have to be, the bound alone decides.
No kernel may reach another device: no remote copies, remote signals or barrier semaphores. Data moves between devices by JAX's collectives and lax.ppermute only.
A program may use at most 128 MiB of HBM per device.

```python
import math
import jax
import jax.numpy as jnp
from jax import lax

D = 512
OUTS = 64
ITERS = 2
ROWS_DEV = 512
SUB = 128
N = 8192
W = 4096
N_CENTRE = 2


latent_rank = 4


floor_ratio = 0.9


latent_ratio = 0.354


def embedding(key):
    embed_key = jax.random.fold_in(key, 7)
    return jax.random.normal(embed_key, (latent_rank, D), jnp.float32) * float(D) ** (-0.5)


def geometry_scale():
    return 0.1 * math.log(float(W)) - 0.04


def manifold_points(key, total_rows, offset_tag):
    scale = geometry_scale()
    point_key = jax.random.fold_in(key, offset_tag)
    latent_key = jax.random.fold_in(point_key, 0)
    noise_key = jax.random.fold_in(point_key, 2)
    latent = jax.random.normal(latent_key, (total_rows, latent_rank), jnp.float32)
    latent = jnp.clip(latent, -6.0, 6.0) * (latent_ratio * scale)
    placed = jnp.dot(latent, embedding(key), precision=jax.lax.Precision.HIGHEST)
    noise = jax.random.normal(noise_key, (total_rows, D), jnp.float32) * (floor_ratio * scale / math.sqrt(2.0 * float(D)))
    return jnp.clip(placed + noise, -4.0, 4.0)


def draw_samples(key, part):
    return manifold_points(key, N, 11)


def draw_centres(key, part):
    return manifold_points(key, W, 13)


def levels(own_key, shape, cuts, smallest, high):
    gain, own = 1.0, jax.random.fold_in(own_key, 6)
    for axis_at, shards_of in cuts:
        steps = jnp.exp(jax.random.uniform(jax.random.fold_in(own, axis_at), (shards_of,), jnp.float32, smallest / len(cuts), high / len(cuts)))
        gain = gain * jnp.repeat(steps, shape[axis_at] // shards_of).reshape([-1 if axis == axis_at else 1 for axis in range(len(shape))])
    return gain


def gaussian(own_key, extent, deviation, bound, shards=(), dtype=jnp.bfloat16):
    loudness = levels(own_key, extent, shards, -0.22, 0.18) if shards else 1.0
    array = jax.random.normal(own_key, extent, jnp.float32) * deviation * loudness
    return jnp.minimum(jnp.maximum(array, -bound), bound).astype(dtype)


def setup_inputs(seed: int = 0) -> dict:
    streams_of = jax.random.split(jax.random.key(seed), 5)
    samples = draw_samples(jax.random.fold_in(streams_of[4], 71), 0)
    targets = gaussian(streams_of[1], (N, OUTS), 1.0, 6.0, ((0, 16),), jnp.float32)
    centres = draw_centres(jax.random.fold_in(streams_of[4], 71), 0)
    coefficients = gaussian(streams_of[3], (W, OUTS), 0.15, 0.9, ((0, 2),), jnp.float32)
    return {"samples": samples, "targets": targets, "centres": centres, "coefficients": coefficients}


softening = 0.01
kernel_scale = 0.2
learning_rate = 4.0

def kernel_block(left, right):
    cross = lax.dot_general(left, right, (((1,), (1,)), ((), ())), precision=lax.Precision.HIGHEST, preferred_element_type=jnp.float32)
    left_sq = lax.optimization_barrier(jnp.sum(left * left, axis=1))
    right_sq = lax.optimization_barrier(jnp.sum(right * right, axis=1))
    dist_sq = jnp.maximum(left_sq[:, None] + right_sq[None, :] - 2.0 * cross, 0.0)
    return jnp.exp(-jnp.sqrt(dist_sq + softening) / kernel_scale)

def matmul(left, right):
    return jnp.dot(left, right, precision=lax.Precision.HIGHEST, preferred_element_type=jnp.float32)

def reference(samples, targets, centres, coefficients):
    row_blocks = samples.reshape(-1, ROWS_DEV, D)
    predictions = lax.map(lambda block: matmul(kernel_block(block, centres), coefficients), row_blocks).reshape(-1, OUTS)
    residual = predictions - targets
    centre_blocks = centres.reshape(-1, SUB * N_CENTRE, D)
    gradient = lax.map(lambda block: matmul(kernel_block(block, samples), residual), centre_blocks).reshape(-1, OUTS)

    def first_pass(block):
        square = kernel_block(block, centres)
        return (lax.optimization_barrier(jnp.sum(square, axis=1)), matmul(square, gradient))
    row_sums, kernel_grad = lax.map(first_pass, centre_blocks)
    step_size = 1.0 / jnp.max(row_sums)
    theta = step_size * gradient
    image = step_size * kernel_grad.reshape(-1, OUTS)
    for turn in range(ITERS):
        if turn > 0:
            current = theta
            image = lax.map(lambda block: matmul(kernel_block(block, centres), current), centre_blocks).reshape(-1, OUTS)
        theta = theta + step_size * (gradient - image)
    return (residual, coefficients - learning_rate * theta)
```

```python
import jax
import jax.numpy as jnp
from jax import lax
from jax.sharding import PartitionSpec as P

softening = 0.01
kernel_scale = 0.2
learning_rate = 4.0
precision = lax.Precision.HIGHEST


def dot(left, right, left_dim, right_dim):
    return lax.dot_general(
        left,
        right,
        (((left_dim,), (right_dim,)), ((), ())),
        precision=precision,
        preferred_element_type=jnp.float32,
    )


def kernel_block(left, right):
    cross = dot(left, right, 1, 1)
    left_sq = jnp.sum(left * left, axis=1)
    right_sq = jnp.sum(right * right, axis=1)
    dist_sq = jnp.maximum(left_sq[:, None] + right_sq[None, :] - 2.0 * cross, 0.0)
    return jnp.exp(-jnp.sqrt(dist_sq + softening) / kernel_scale)


def send_xor(array, mask):
    count = lax.axis_size("dp")
    return lax.ppermute(array, "dp", [(i, i ^ mask) for i in range(count)])


def send_far(array, mask, shift):
    dp, centre = lax.axis_size("dp"), lax.axis_size("centre")
    pairs = [
        (d * centre + c, (d ^ mask) * centre + (c + shift) % centre)
        for d in range(dp)
        for c in range(centre)
    ]
    return lax.ppermute(array, ("dp", "centre"), pairs)


def body(samples, targets, centres, coefficients):
    count = lax.axis_size("dp")
    shards = lax.axis_size("centre")
    index = lax.axis_index("dp")
    shard = lax.axis_index("centre")
    share = centres.shape[0] // count
    outs = targets.shape[1]
    half = count // 2
    mids = half // 2
    core = index % 2
    mid = (index // 2) % mids
    top = index // half

    blocks = centres.reshape(2, mids, 2, share, centres.shape[1])
    own = lax.dynamic_slice(blocks, (0, mid, core, 0, 0), (2, 1, 1, share, centres.shape[1]))
    own = own.reshape(2, share, centres.shape[1])
    mine = lax.dynamic_index_in_dim(own, top, 0, keepdims=False)
    far = [send_far(mine, 0, -shift) for shift in range(1, shards)]
    data_tile = kernel_block(samples, centres)
    partial_pred = dot(data_tile, coefficients, 1, 0)
    other = [send_xor(block, half) for block in far]
    predictions = partial_pred
    for shift in range(1, shards):
        predictions = predictions + send_far(partial_pred, 0, shift)
    residual = predictions - targets
    grad = dot(residual, data_tile, 0, 0)
    grad = grad.reshape(outs, 2, mids, 2, share)

    def scatter(partial):
        keep = lax.dynamic_index_in_dim(partial, core, 3, keepdims=False)
        give = lax.dynamic_index_in_dim(partial, 1 - core, 3, keepdims=False)
        part = keep + send_xor(give, 1)
        pieces = [lax.dynamic_index_in_dim(part, mid ^ m, 2, keepdims=False) for m in range(mids)]
        total = pieces[0]
        for m in range(1, mids):
            total = total + send_xor(pieces[m], 2 * m)
        return total

    part = scatter(grad)

    row_blocks = [own[top], own[1 - top]]
    for block, twin in zip(far, other):
        row_blocks += [block, twin]
    rows = jnp.concatenate(row_blocks, axis=0)
    square = kernel_block(centres, rows)
    row_part = jnp.sum(square, axis=0)

    gathered = [part] + [send_xor(part, 2 * m) for m in range(1, mids)]
    gathered = [(piece, send_xor(piece, 1)) for piece in gathered]
    full = jnp.zeros((outs, 2, mids, 2, share), jnp.float32)
    for m in range(mids):
        for k in range(2):
            full = lax.dynamic_update_slice(
                full, gathered[m][k][:, :, None, None, :], (0, 0, mid ^ m, core ^ k, 0)
            )
    image = dot(full.reshape(outs, -1), square, 1, 0).reshape(outs, shards, 2, share)
    near, away = image[:, :, 0], image[:, :, 1]

    def turn(blocks, shift):
        return jnp.roll(blocks, shift, axis=1)

    total = near
    sums = row_part.reshape(shards, 2 * share)
    row_sums = sums
    for shift in range(shards):
        total = total + turn(send_far(away, half, shift), -shift)
        if shift:
            total = total + turn(send_far(near, 0, shift), -shift)
            row_sums = row_sums + jnp.roll(send_far(sums, 0, shift), -shift, axis=0)
    largest = jnp.max(row_sums).reshape(1, 1)
    near_square = square.reshape(-1, shards, 2, share)[:, :, 0].reshape(-1, shards * share)
    second = dot(total.reshape(outs, -1), near_square, 1, 1)
    second = scatter(second.reshape(outs, 2, mids, 2, share))
    largest = jnp.maximum(largest, send_xor(largest, 1))
    best = largest
    for m in range(1, mids):
        best = jnp.maximum(best, send_xor(largest, 2 * m))
    step = 1.0 / best[0, 0]
    partial = 3.0 * step * part + step * step * step * second
    theta = partial[:, top] + send_xor(partial[:, 1 - top], half)
    theta = theta - 3.0 * step * step * total[:, 0]
    own_coeffs = lax.dynamic_slice_in_dim(coefficients, index * share, share, 0)
    return (residual, own_coeffs - learning_rate * theta.T)


def solution(mesh):
    return jax.shard_map(
        body,
        mesh=mesh,
        in_specs=(P("dp", None), P("dp", None), P("centre", None), P("centre", None)),
        out_specs=(P("dp", None), P(("centre", "dp"), None)),
        check_vma=False,
    )
```

```python
import functools
import jax
import jax.numpy as jnp
from jax import lax
from jax.experimental import pallas as pl
from jax.experimental.pallas import tpu as pltpu
from jax.sharding import PartitionSpec as P

softening = 0.01
kernel_scale = 0.2
learning_rate = 4.0
f32, bf16 = jnp.float32, jnp.bfloat16


def split(x):
    high = x.astype(bf16)
    return high, (x - high.astype(f32)).astype(bf16)


def dot(left, right):
    return jnp.dot(left, right, preferred_element_type=f32)


def add(ref, value, step):
    ref[...] = jnp.where(step == 0, value, ref[...] + value)


def call(kernel, name, info, ins, outs, grid=(1,), scratch=(), flops=0, size=0, room=16):
    def spec(pair):
        array, block = pair
        if block is None:
            rank = len(array.shape)
            return pl.BlockSpec(array.shape, lambda i, s, rank=rank: (0,) * rank)
        return pl.BlockSpec(*block)

    result = pl.pallas_call(
        kernel,
        name=name,
        grid_spec=pltpu.PrefetchScalarGridSpec(
            num_scalar_prefetch=1,
            grid=grid,
            in_specs=[spec(pair) for pair in ins],
            out_specs=[spec(pair) for pair in outs],
            scratch_shapes=list(scratch),
        ),
        out_shape=[jax.ShapeDtypeStruct(a.shape, a.dtype) for a, _ in outs],
        compiler_params=pltpu.CompilerParams(vmem_limit_bytes=room * 1024 * 1024),
        cost_estimate=pl.CostEstimate(flops=flops, bytes_accessed=size, transcendentals=0),
    )(info, *[array for array, _ in ins])
    return result


def like(*shape, dtype=f32):
    return jax.ShapeDtypeStruct(shape, dtype)


def points_in(x, at, high_ref, low_ref, square_ref):
    xt = x.T
    high, low = split(xt)
    wide, rest = high.astype(f32), low.astype(f32)
    where = pl.ds(at, x.shape[0])
    square_ref[:, where] = jnp.sum(wide * wide + 2.0 * (wide * rest), axis=0, keepdims=True)
    high_ref[:, where] = (-2.0 * wide).astype(bf16)
    low_ref[:, where] = (-2.0 * rest).astype(bf16)


def entries(high, low, square, xh, xl, xsq):
    cross = dot(high, xh) + dot(low, xh) + dot(high, xl)
    dist = jnp.maximum(cross + (square + xsq), 0.0) + softening
    return jnp.exp(jnp.sqrt(dist) * (-1.0 / kernel_scale))


def data_kernel(info, x_ref, c_ref, w_ref, *refs):
    near_ref, away_ref, kh_ref, kl_ref, ch_ref, cl_ref, sq_ref, pred_ref, rows_ref, xh, xl, xsq, acc = refs
    step = pl.program_id(0)

    @pl.when(step == 0)
    def _():
        points_in(x_ref[...], 0, xh, xl, xsq)
        share = near_ref.shape[0]
        rows_ref[:share, :] = near_ref[...]
        rows_ref[share:, :] = away_ref[...]

    high, low = split(c_ref[...])
    wide, rest = high.astype(f32), low.astype(f32)
    square = jnp.sum(wide * wide + 2.0 * (wide * rest), axis=1, keepdims=True)
    ch_ref[...] = high
    cl_ref[...] = low
    sq_ref[...] = square
    tile = entries(high, low, square, xh[...], xl[...], xsq[...])
    kh, kl = split(tile)
    kh_ref[...] = kh
    kl_ref[...] = kl
    weights = jnp.concatenate(split(w_ref[...]), axis=0)
    add(acc, dot(weights, kh) + dot(weights, kl), step)
    outs = pred_ref.shape[0]

    @pl.when(step == pl.num_programs(0) - 1)
    def _():
        pred_ref[...] = acc[:outs, :] + acc[outs:, :]


def centre_kernel(info, *refs):
    x_refs = refs[:-9]
    ch_ref, cl_ref, sq_ref, kh_ref, kl_ref, sum_ref, xh, xl, xsq = refs[-9:]
    step = pl.program_id(0)

    @pl.when(step == 0)
    def _():
        at = 0
        for x_ref in x_refs:
            points_in(x_ref[...], at, xh, xl, xsq)
            at += x_ref.shape[0]

    tile = entries(ch_ref[...], cl_ref[...], sq_ref[...], xh[...], xl[...], xsq[...])
    kh, kl = split(tile)
    kh_ref[...] = kh
    kl_ref[...] = kl
    add(sum_ref, jnp.sum(tile.reshape(-1, 8, tile.shape[1]), axis=0), step)


def back(parts, right, out_ref):
    points = sum(ref.shape[-1] for ref in parts[0])
    high, low = [
        jnp.concatenate([ref[...].reshape(-1, ref.shape[-1]) for ref in refs], axis=1) for refs in parts
    ]
    outs = right.shape[1] // 2
    product = (dot(high, right) + dot(low, right)).T
    out_ref[:outs, :] = product[:outs] + product[outs:]


def grad_kernel(others, info, *refs):
    p_refs = refs[: 1 + others]
    t_ref, high_ref, low_ref, out_ref, res_ref, right_ref = refs[1 + others :]

    @pl.when(pl.program_id(0) == 0)
    def _():
        total = p_refs[0][...]
        for ref in p_refs[1:]:
            total = total + ref[...]
        residual = total - t_ref[...]
        res_ref[...] = residual
        right_ref[...] = jnp.concatenate(split(residual.T), axis=1)

    back(([high_ref], [low_ref]), right_ref[...], out_ref)


def keep_kernel(info, right_ref, *refs):
    count = len(refs) // 2
    back((refs[:count], refs[count:-1]), right_ref[...], refs[-1])


def image_kernel(shards, info, *refs):
    near_refs, away_refs = refs[:shards], refs[shards : 2 * shards]
    high_refs, low_refs = refs[2 * shards : 3 * shards], refs[3 * shards : 4 * shards]
    out_ref, right_ref, own_ref, max_ref, image_ref = refs[4 * shards :]
    outs, share = own_ref.shape

    @pl.when(pl.program_id(0) == 0)
    def _():
        total = near_refs[0][...]
        for ref in near_refs[1:]:
            total = total + ref[...]
        image = total[:outs]
        for ref in away_refs:
            image = image + ref[...]
        largest = jnp.max(total[outs : outs + 2], keepdims=True)
        max_ref[...] = jnp.broadcast_to(largest, max_ref.shape)
        image_ref[...] = image
        for j in range(shards):
            part = image_ref[:, pl.ds(place(info, j, shards, share), share)]
            right_ref[j * share : (j + 1) * share, :] = jnp.concatenate(split(part.T), axis=1)
            if j == 0:
                own_ref[...] = part

    back((high_refs, low_refs), right_ref[...], out_ref)
    out_ref[outs:, :] = jnp.broadcast_to(max_ref[:, :1], (8, out_ref.shape[1]))


def place(info, j, shards, share):
    return pl.multiple_of(lax.rem(info[3] + j, shards) * share, share)


def product_kernel(mids, shards, info, *refs):
    pieces = refs[: 2 * mids]
    oh, ol, fh, fl, osum, fsum, near_ref, away_ref, left, own, far = refs[2 * mids :]
    outs = pieces[0].shape[0]
    share = pieces[0].shape[1] // 2
    step = pl.program_id(0)

    @pl.when(step == 0)
    def _():
        core, mid = info[0], info[1]
        for m in range(mids):
            for k in range(2):
                high, low = split(pieces[2 * m + k][...])
                for top in range(2):
                    block = top * 2 * mids + 2 * (mid ^ m) + (core ^ k)
                    where = pl.ds(pl.multiple_of(block * share, share), share)
                    left[:outs, where] = high[:, top * share : (top + 1) * share]
                    left[outs:, where] = low[:, top * share : (top + 1) * share]

    rows = oh.shape[0]
    part = left[:, pl.ds(pl.multiple_of(step * rows, rows), rows)]
    add(own, dot(part, oh[...]) + dot(part, ol[...]), step)
    add(far, dot(part, fh[...]) + dot(part, fl[...]), step)

    @pl.when(step == pl.num_programs(0) - 1)
    def _():
        row = lax.broadcasted_iota(jnp.int32, (8, share), 0)
        for j in range(shards):
            source, sums, at = (own, osum, 0) if j == 0 else (far, fsum, 2 * share * (j - 1))
            where = pl.ds(place(info, j, shards, share), share)
            first, last = slice(at, at + share), slice(at + share, at + 2 * share)
            near_ref[:outs, where] = source[:outs, first] + source[outs:, first]
            away_ref[:, where] = source[:outs, last] + source[outs:, last]
            near_sum = jnp.sum(sums[:, first], axis=0, keepdims=True)
            away_sum = jnp.sum(sums[:, last], axis=0, keepdims=True)
            near_ref[outs:, where] = jnp.where(row == 0, near_sum, away_sum)


def join_kernel(mids, share, info, keep_ref, got_ref, *refs):
    outs = keep_ref.shape[0]
    piece_refs = refs[-mids:]
    for m in range(mids):
        for top in range(2):
            at = pl.ds(pl.multiple_of((top * mids + (info[1] ^ m)) * share, share), share)
            to = slice(top * share, (top + 1) * share)
            piece_refs[m][:outs, to] = keep_ref[:, at] + got_ref[:outs, at]
    if len(refs) > mids:
        largest = jnp.maximum(refs[0][...], got_ref[outs:, : refs[0].shape[1]])
        for m in range(mids):
            piece_refs[m][outs:, :] = jnp.broadcast_to(largest[:, :1], (8, 2 * share))


def sum_kernel(info, *refs):
    total = refs[0][...]
    for ref in refs[1:-1]:
        total = total + ref[...]
    refs[-1][...] = total


def theta_kernel(mids, share, info, part_ref, own_ref, *refs):
    pieces = refs[:mids]
    keep_ref, give_ref = refs[mids:]
    outs = part_ref.shape[0]
    second = pieces[0][:outs, :]
    largest = pieces[0][outs:, :]
    for ref in pieces[1:]:
        second = second + ref[:outs, :]
        largest = jnp.maximum(largest, ref[outs:, :])
    step = 1.0 / largest[:1, :1]
    theta = (3.0 * step) * part_ref[...] + (step * step * step) * second
    first, last = theta[:, :share], theta[:, share:]
    upper = info[2] == 1
    keep_ref[...] = jnp.where(upper, last, first) - (3.0 * step * step) * own_ref[...]
    give_ref[...] = jnp.where(upper, first, last)


def final_kernel(info, keep_ref, got_ref, coeff_ref, out_ref):
    out_ref[...] = coeff_ref[...] - learning_rate * (keep_ref[...] + got_ref[...])


def send_xor(array, mask):
    count = lax.axis_size("dp")
    return lax.ppermute(array, "dp", [(i, i ^ mask) for i in range(count)])


def send_far(array, mask, shift):
    dp, centre = lax.axis_size("dp"), lax.axis_size("centre")
    pairs = [
        (d * centre + c, (d ^ mask) * centre + (c + shift) % centre)
        for d in range(dp)
        for c in range(centre)
    ]
    return lax.ppermute(array, ("dp", "centre"), pairs)


def after(value, *others):
    return lax.optimization_barrier((value, *others))[0]


def body(samples, targets, centres, coefficients):
    count = lax.axis_size("dp")
    shards = lax.axis_size("centre")
    index = lax.axis_index("dp")
    rows, width = centres.shape
    share = rows // count
    points, outs = targets.shape
    half = count // 2
    mids = half // 2
    core, mid, top = index % 2, (index // 2) % mids, index // half
    info = jnp.stack([core, mid, top, lax.axis_index("centre"), index, index ^ half]).astype(jnp.int32)
    weights = coefficients.T

    near = (centres, ((share, width), lambda i, s: (s[4], 0)))
    away = (centres, ((share, width), lambda i, s: (s[5], 0)))
    block = min(512, rows)
    steps = rows // block
    rowed = lambda array, wide: (array, ((block, wide), lambda i, s: (i, 0)))
    kh, kl, ch, cl, square, pred, pair = call(
        data_kernel, "data", info,
        [(samples, None), rowed(centres, width), (weights, ((outs, block), lambda i, s: (0, i))), near, away],
        [
            rowed(like(rows, points, dtype=bf16), points),
            rowed(like(rows, points, dtype=bf16), points),
            rowed(like(rows, width, dtype=bf16), width),
            rowed(like(rows, width, dtype=bf16), width),
            rowed(like(rows, 1), 1),
            (like(outs, points), None),
            (like(2 * share, width), None),
        ],
        (steps,),
        [
            pltpu.VMEM((width, points), bf16),
            pltpu.VMEM((width, points), bf16),
            pltpu.VMEM((1, points), f32),
            pltpu.VMEM((2 * outs, points), f32),
        ],
        flops=6 * rows * points * width, size=12 * rows * width,
    )
    got = [send_far(pred, 0, shift) for shift in range(1, shards)]

    def centre_tile(blocks, columns, name):
        return call(
            centre_kernel, name, info,
            blocks + [rowed(ch, width), rowed(cl, width), rowed(square, 1)],
            [
                rowed(like(rows, columns, dtype=bf16), columns),
                rowed(like(rows, columns, dtype=bf16), columns),
                (like(8, columns), None),
            ],
            (steps,),
            [
                pltpu.VMEM((width, columns), bf16),
                pltpu.VMEM((width, columns), bf16),
                pltpu.VMEM((1, columns), f32),
            ],
            flops=6 * rows * columns * width, size=8 * rows * width,
            room=12 + columns // 64,
        )

    own_high, own_low, own_sums = centre_tile([near, away], 2 * share, "own_tile")
    far = [send_far(after(pair, own_high), 0, -shift) for shift in range(1, shards)]
    got[0] = after(got[0], own_high)

    pairs = count // 2
    group = min(4, pairs)

    def halves(array, flip, wide, at=0):
        return (
            array.reshape(pairs, 2, share, array.shape[1]),
            ((group, None, share, wide), lambda i, s: (i, s[0] ^ flip, 0, at)),
        )

    def columns(height):
        return (like(height, pairs * share), ((height, group * share), lambda i, s: (0, i)))

    backs = (pairs // group,)
    give, residual, right = call(
        functools.partial(grad_kernel, len(got)), "grad_give", info,
        [(pred, None)]
        + [(g, None) for g in got]
        + [(targets.T, None), halves(kh, 1, points), halves(kl, 1, points)],
        [columns(outs), (like(outs, points), None), (like(points, 2 * outs, dtype=bf16), None)],
        backs,
    )
    received = send_xor(give, 1)
    (keep,) = call(
        keep_kernel, "grad_keep", info,
        [(right, None), halves(kh, 0, points), halves(kl, 0, points)],
        [columns(outs)], backs,
    )

    def join(keep, received, extra, height):
        return call(
            functools.partial(join_kernel, mids, share), "join", info,
            [(keep, None), (received, None)] + [(e, None) for e in extra],
            [(like(height, 2 * share), None)] * mids,
        )

    pieces = join(keep, received, [], outs)
    pieces = [pieces[0]] + [send_xor(pieces[m], 2 * m) for m in range(1, mids)]
    (part,) = call(
        sum_kernel, "sum", info, [(p, None) for p in pieces], [(like(outs, 2 * share), None)]
    )
    gathered = [part] + [send_xor(part, 2 * m) for m in range(1, mids)]
    parts = []
    for piece in gathered:
        parts += [piece, send_xor(piece, 1)]
    wide = 2 * share * (shards - 1)
    far_high, far_low, far_sums = centre_tile([(after(f, part), None) for f in far], wide, "far_tile")

    near_part, away_part = call(
        functools.partial(product_kernel, mids, shards), "product", info,
        [(p, None) for p in parts]
        + [rowed(own_high, 2 * share), rowed(own_low, 2 * share), rowed(far_high, wide), rowed(far_low, wide)]
        + [(own_sums, None), (far_sums, None)],
        [(like(outs + 8, shards * share), None), (like(outs, shards * share), None)],
        (steps,),
        [
            pltpu.VMEM((2 * outs, rows), bf16),
            pltpu.VMEM((2 * outs, 2 * share), f32),
            pltpu.VMEM((2 * outs, wide), f32),
        ],
        room=12 + wide // 64,
    )
    nears = [near_part] + [send_far(near_part, 0, shift) for shift in range(1, shards)]
    aways = [send_far(away_part, half, shift) for shift in range(shards)]

    def near_halves(own, far, flip):
        return [halves(own, flip, share)] + [halves(far, flip, share, 2 * j) for j in range(shards - 1)]

    give, right, own, largest = call(
        functools.partial(image_kernel, shards), "image_give", info,
        [(a, None) for a in nears + aways]
        + near_halves(own_high, far_high, 1)
        + near_halves(own_low, far_low, 1),
        [
            columns(outs + 8),
            (like(shards * share, 2 * outs, dtype=bf16), None),
            (like(outs, share), None),
            (like(8, share), None),
        ],
        backs, [pltpu.VMEM((outs, shards * share), f32)],
    )
    received = send_xor(give, 1)
    (keep,) = call(
        keep_kernel, "image_keep", info,
        [(right, None)] + near_halves(own_high, far_high, 0) + near_halves(own_low, far_low, 0),
        [columns(outs)], backs,
    )
    pieces = join(keep, received, [largest], outs + 8)
    pieces = [pieces[0]] + [send_xor(pieces[m], 2 * m) for m in range(1, mids)]
    keep, give = call(
        functools.partial(theta_kernel, mids, share), "theta", info,
        [(part, None), (own, None)] + [(p, None) for p in pieces],
        [(like(outs, share), None)] * 2,
    )
    (new_coefficients,) = call(
        final_kernel, "final", info,
        [
            (keep, None),
            (send_xor(give, half), None),
            (weights, ((outs, share), lambda i, s: (0, s[4]))),
        ],
        [(like(outs, share), None)],
    )
    return (residual.T, new_coefficients.T)


def solution(mesh):
    return jax.shard_map(
        body,
        mesh=mesh,
        in_specs=(P("dp", None), P("dp", None), P("centre", None), P("centre", None)),
        out_specs=(P("dp", None), P(("centre", "dp"), None)),
        check_vma=False,
    )
```

```python
import functools
import jax
import jax.numpy as jnp
from jax import lax
from jax.experimental import pallas as pl
from jax.experimental.pallas import tpu as pltpu
from jax.sharding import PartitionSpec as P

softening = 0.01
kernel_scale = 0.2
learning_rate = 4.0
f32, bf16 = jnp.float32, jnp.bfloat16
mega = 1024 * 1024


def split(x):
    high = x.astype(bf16)
    return high, (x - high.astype(f32)).astype(bf16)


def dot(left, right):
    return jnp.dot(left, right, preferred_element_type=f32)


def place():
    index, count = lax.axis_index("dp"), lax.axis_size("dp")
    return index, lax.rem(index, 2), lax.rem(index // 2, count // 4), index // (count // 2)


def like(*shape, dtype=f32):
    return jax.ShapeDtypeStruct(shape, dtype)


def call(kernel, name, ins, outs, scratch=(), room=8 * mega, flops=0, space=pltpu.VMEM):
    return pl.pallas_call(
        kernel,
        name=name,
        in_specs=[pl.BlockSpec(memory_space=space)] * len(ins),
        out_specs=[pl.BlockSpec(memory_space=pltpu.VMEM)] * len(outs),
        out_shape=list(outs),
        scratch_shapes=list(scratch),
        compiler_params=pltpu.CompilerParams(vmem_limit_bytes=room),
        cost_estimate=pl.CostEstimate(flops=flops, bytes_accessed=0, transcendentals=0),
    )(*ins)


def points_in(x):
    high, low = split(x.T)
    wide, rest = high.astype(f32), low.astype(f32)
    square = jnp.sum(wide * wide + 2.0 * (wide * rest), axis=0, keepdims=True)
    return (-2.0 * wide).astype(bf16), (-2.0 * rest).astype(bf16), square


def entries(high, low, square, xh, xl, xsq):
    cross = dot(high, xh) + dot(low, xh) + dot(high, xl)
    dist = jnp.maximum(cross + (square + xsq), 0.0) + softening
    return jnp.exp(dist * lax.rsqrt(dist) * (-1.0 / kernel_scale))


def load_kernel(c_hbm, ch_ref, cl_ref, sq_ref, pair_ref, c_ref, sems):
    rows, share = c_ref.shape[0], pair_ref.shape[0] // 2
    index, half = place()[0], lax.axis_size("dp") // 2
    loads = sems.shape[0]
    load = rows // loads
    copies = [
        pltpu.make_async_copy(c_hbm.at[pl.ds(i * load, load)], c_ref.at[pl.ds(i * load, load)], sems.at[i])
        for i in range(loads)
    ]
    for copy in copies:
        copy.start()
    for i, copy in enumerate(copies):
        copy.wait()
        where = slice(i * load, (i + 1) * load)
        high, low = split(c_ref[where, :])
        wide, rest = high.astype(f32), low.astype(f32)
        ch_ref[where, :] = high
        cl_ref[where, :] = low
        sq_ref[where, :] = jnp.sum(wide * wide + 2.0 * (wide * rest), axis=1, keepdims=True)
    for t, at in enumerate((index, lax.rem(index + half, 2 * half))):
        pair_ref[t * share : (t + 1) * share, :] = c_ref[pl.ds(pl.multiple_of(at * share, share), share), :]


def data_kernel(block, x_ref, w_ref, ch_ref, cl_ref, sq_ref, kh_ref, kl_ref, pred_ref, xh_ref, xl_ref):
    rows, outs = ch_ref.shape[0], pred_ref.shape[0]
    xh, xl, xsq = points_in(x_ref[...])
    xh_ref[...] = xh
    xl_ref[...] = xl
    pred = None
    for i in range(rows // block):
        where = slice(i * block, (i + 1) * block)
        tile = entries(ch_ref[where, :], cl_ref[where, :], sq_ref[where, :], xh_ref[...], xl_ref[...], xsq)
        kh, kl = split(tile)
        kh_ref[where, :] = kh
        kl_ref[where, :] = kl
        weights = jnp.concatenate(split(w_ref[:, where]), axis=0)
        part = dot(weights, kh) + dot(weights, kl)
        pred = part if pred is None else pred + part
    pred_ref[...] = pred[:outs, :] + pred[outs:, :]


def centre_kernel(block, *refs):
    x_refs = refs[:-8]
    ch_ref, cl_ref, sq_ref, kh_ref, kl_ref, sum_ref, xh_ref, xl_ref = refs[-8:]
    rows = ch_ref.shape[0]
    at = 0
    for x_ref in x_refs:
        span = slice(at, at + x_ref.shape[0])
        at = span.stop
        xh, xl, xsq = points_in(x_ref[...])
        xh_ref[...] = xh
        xl_ref[...] = xl
        total = None
        for i in range(rows // block):
            where = slice(i * block, (i + 1) * block)
            tile = entries(ch_ref[where, :], cl_ref[where, :], sq_ref[where, :], xh_ref[...], xl_ref[...], xsq)
            kh, kl = split(tile)
            kh_ref[where, span] = kh
            kl_ref[where, span] = kl
            part = jnp.sum(tile.reshape(-1, 8, tile.shape[1]), axis=0)
            total = part if total is None else total + part
        sum_ref[:, span] = total


def share_rows(mids, share, flip):
    _, core, mid, _ = place()
    for m in range(mids):
        for top in range(2):
            block = top * 2 * mids + 2 * (mid ^ m) + (core ^ flip)
            yield pl.ds(pl.multiple_of(block * share, share), share)


def take(ref, where, columns=slice(None)):
    return jnp.concatenate([ref[rows, columns] for rows in where], axis=0)


def back(mids, share, flip, parts, right):
    where = list(share_rows(mids, share, flip))
    product, at = 0.0, 0
    for high, low, columns in parts:
        size = columns.stop - columns.start
        values = right[at : at + size]
        at += size
        product = product + (dot(take(high, where, columns), values) + dot(take(low, where, columns), values))
    product = product.T
    outs = right.shape[1] // 2
    return product[:outs] + product[outs:]


def grad_kernel(mids, share, *refs):
    t_ref, high_ref, low_ref, out_ref, res_ref, right_ref = refs[-6:]
    total = refs[0][...]
    for ref in refs[1:-6]:
        total = total + ref[...]
    residual = total - t_ref[...]
    res_ref[...] = residual
    right = jnp.concatenate(split(residual.T), axis=1)
    right_ref[...] = right
    out_ref[...] = back(mids, share, 1, [(high_ref, low_ref, slice(0, right.shape[0]))], right)


def grad_keep_kernel(mids, share, right_ref, high_ref, low_ref, out_ref):
    right = right_ref[...]
    out_ref[...] = back(mids, share, 0, [(high_ref, low_ref, slice(0, right.shape[0]))], right)


def near_parts(share, own_high, own_low, far_high, far_low):
    parts = [(own_high, own_low, slice(0, share))]
    for at in range(0, far_high.shape[1], 2 * share):
        parts.append((far_high, far_low, slice(at, at + share)))
    return parts


def image_kernel(mids, shards, *refs):
    near_refs, away_refs = refs[:shards], refs[shards : 2 * shards]
    kernels = refs[2 * shards : 2 * shards + 4]
    out_ref, right_ref, own_ref, max_ref, image_ref = refs[2 * shards + 4 :]
    outs, share = own_ref.shape
    total = near_refs[0][...]
    for ref in near_refs[1:]:
        total = total + ref[...]
    image = total[:outs]
    for ref in away_refs:
        image = image + ref[...]
    largest = jnp.max(total[outs : outs + 2], keepdims=True)
    max_ref[...] = jnp.broadcast_to(largest, max_ref.shape)
    out_ref[outs:, :] = jnp.broadcast_to(largest, (8, out_ref.shape[1]))
    image_ref[...] = image
    for j in range(shards):
        part = image_ref[:, pl.ds(shard_at(j, shards, share), share)]
        right_ref[j * share : (j + 1) * share, :] = jnp.concatenate(split(part.T), axis=1)
        if j == 0:
            own_ref[...] = part
    out_ref[:outs, :] = back(mids, share, 1, near_parts(share, *kernels), right_ref[...])


def image_keep_kernel(mids, share, right_ref, *refs):
    refs[-1][...] = back(mids, share, 0, near_parts(share, *refs[:4]), right_ref[...])


def shard_at(j, shards, share):
    return pl.multiple_of(lax.rem(lax.axis_index("centre") + j, shards) * share, share)


def product(mids, share, flip, pieces, kernels):
    where = list(share_rows(mids, share, flip))
    high, low = split(jnp.concatenate([ref[...] for ref in pieces], axis=1))
    left = jnp.concatenate([high, low], axis=0)
    outs = high.shape[0]
    for kh, kl in (kernels[:2], kernels[2:]):
        result = dot(left, take(kh, where)) + dot(left, take(kl, where))
        yield result[:outs] + result[outs:]


def first_kernel(mids, share, *refs):
    own_ref, far_ref = refs[-2:]
    own, far = product(mids, share, 0, refs[:mids], refs[mids : mids + 4])
    own_ref[...] = own
    far_ref[...] = far


def second_kernel(mids, shards, *refs):
    own_ref, far_ref, osum, fsum, near_ref, away_ref = refs[mids + 4 :]
    outs = away_ref.shape[0]
    share = away_ref.shape[1] // shards
    own, far = product(mids, share, 1, refs[:mids], refs[mids : mids + 4])
    own, far = own + own_ref[...], far + far_ref[...]
    row = lax.broadcasted_iota(jnp.int32, (8, share), 0)
    for j in range(shards):
        source, sums, at = (own, osum, 0) if j == 0 else (far, fsum, 2 * share * (j - 1))
        where = pl.ds(shard_at(j, shards, share), share)
        first, last = slice(at, at + share), slice(at + share, at + 2 * share)
        near_ref[:outs, where] = source[:, first]
        away_ref[:, where] = source[:, last]
        near_sum = jnp.sum(sums[:, first], axis=0, keepdims=True)
        away_sum = jnp.sum(sums[:, last], axis=0, keepdims=True)
        near_ref[outs:, where] = jnp.where(row == 0, near_sum, away_sum)


def join_kernel(mids, keep_ref, got_ref, *refs):
    outs = keep_ref.shape[0]
    piece_refs = refs[-mids:]
    wide = piece_refs[0].shape[1]
    for m in range(mids):
        columns = slice(m * wide, (m + 1) * wide)
        piece_refs[m][:outs, :] = keep_ref[:, columns] + got_ref[:outs, columns]
    if len(refs) > mids:
        largest = jnp.maximum(refs[0][...], got_ref[outs:, : refs[0].shape[1]])
        for m in range(mids):
            piece_refs[m][outs:, :] = jnp.broadcast_to(largest[:, :1], (8, wide))


def sum_kernel(*refs):
    total = refs[0][...]
    for ref in refs[1:-1]:
        total = total + ref[...]
    refs[-1][...] = total


def theta_kernel(mids, share, part_ref, own_ref, *refs):
    pieces = refs[:mids]
    keep_ref, give_ref = refs[mids:]
    outs = part_ref.shape[0]
    second = pieces[0][:outs, :]
    largest = pieces[0][outs:, :]
    for ref in pieces[1:]:
        second = second + ref[:outs, :]
        largest = jnp.maximum(largest, ref[outs:, :])
    step = 1.0 / largest[:1, :1]
    theta = (3.0 * step) * part_ref[...] + (step * step * step) * second
    first, last = theta[:, :share], theta[:, share:]
    upper = place()[3] == 1
    keep_ref[...] = jnp.where(upper, last, first) - (3.0 * step * step) * own_ref[...]
    give_ref[...] = jnp.where(upper, first, last)


def final_kernel(keep_ref, got_ref, coeff_ref, out_ref):
    share = out_ref.shape[1]
    coefficients = coeff_ref[:, pl.ds(pl.multiple_of(place()[0] * share, share), share)]
    out_ref[...] = coefficients - learning_rate * (keep_ref[...] + got_ref[...])


def send_xor(array, mask):
    count = lax.axis_size("dp")
    return lax.ppermute(array, "dp", [(i, i ^ mask) for i in range(count)])


def send_far(array, mask, shift):
    dp, centre = lax.axis_size("dp"), lax.axis_size("centre")
    pairs = [
        (d * centre + c, (d ^ mask) * centre + (c + shift) % centre)
        for d in range(dp)
        for c in range(centre)
    ]
    return lax.ppermute(array, ("dp", "centre"), pairs)


def after(value, *others):
    return lax.optimization_barrier((value, *others))[0]


def body(samples, targets, centres, coefficients):
    count = lax.axis_size("dp")
    shards = lax.axis_size("centre")
    rows, width = centres.shape
    share = rows // count
    points, outs = targets.shape
    half = count // 2
    mids = half // 2
    weights = coefficients.T
    block = min(256, rows)

    loads = min(8, count)
    kept = 4 * rows * width + 512 * rows + 8 * share * width
    ch, cl, square, pair = call(
        load_kernel, "load", [centres],
        [
            like(rows, width, dtype=bf16),
            like(rows, width, dtype=bf16),
            like(rows, 1),
            like(2 * share, width),
        ],
        [pltpu.VMEM((rows, width), f32), pltpu.SemaphoreType.DMA((loads,))],
        room=103 * mega // 2 - kept, space=pltpu.HBM,
    )
    kh, kl, pred = call(
        functools.partial(data_kernel, block), "data", [samples, weights, ch, cl, square],
        [like(rows, points, dtype=bf16), like(rows, points, dtype=bf16), like(outs, points)],
        [pltpu.VMEM((width, points), bf16), pltpu.VMEM((width, points), bf16)],
    )
    got = [send_far(pred, 0, shift) for shift in range(1, shards)]

    def centre_tile(blocks, name):
        size = blocks[0].shape[0]
        columns = size * len(blocks)
        return call(
            functools.partial(centre_kernel, block), name, blocks + [ch, cl, square],
            [like(rows, columns, dtype=bf16), like(rows, columns, dtype=bf16), like(8, columns)],
            [pltpu.VMEM((width, size), bf16), pltpu.VMEM((width, size), bf16)],
            flops=6 * rows * columns * width,
        )

    own_high, own_low, own_sums = centre_tile([after(pair, pred)], "own_tile")
    got[0] = after(got[0], own_high)

    give, residual, right = call(
        functools.partial(grad_kernel, mids, share), "grad_give",
        [pred] + got + [targets.T, kh, kl],
        [like(outs, half * share), like(outs, points), like(points, 2 * outs, dtype=bf16)],
    )
    received = send_xor(give, 1)
    far = [send_far(after(pair, give), 0, -shift) for shift in range(1, shards)]
    (keep,) = call(
        functools.partial(grad_keep_kernel, mids, share), "grad_keep",
        [right, kh, kl], [like(outs, half * share)],
    )

    def join(keep, received, extra, height):
        return call(
            functools.partial(join_kernel, mids), "join",
            [keep, received] + extra, [like(height, 2 * share)] * mids,
        )

    pieces = join(keep, received, [], outs)
    pieces = [pieces[0]] + [send_xor(pieces[m], 2 * m) for m in range(mids - 1, 0, -1)]
    (part,) = call(sum_kernel, "sum", pieces, [like(outs, 2 * share)])
    gathered = [part] + [send_xor(part, 2 * m) for m in range(1, mids)]
    far_high, far_low, far_sums = centre_tile([after(f, part) for f in far], "far_tile")
    kernels = [own_high, own_low, far_high, far_low]
    crossed = [send_xor(after(piece, far_sums), 1) for piece in gathered]
    wide = 2 * share * (shards - 1)
    firsts = call(
        functools.partial(first_kernel, mids, share), "product_first",
        gathered + kernels, [like(outs, 2 * share), like(outs, wide)],
    )
    near_part, away_part = call(
        functools.partial(second_kernel, mids, shards), "product_second",
        crossed + kernels + list(firsts) + [own_sums, far_sums],
        [like(outs + 8, shards * share), like(outs, shards * share)],
    )
    aways = [send_far(away_part, half, shift) for shift in range(shards - 1, -1, -1)]
    nears = [near_part] + [send_far(near_part, 0, shift) for shift in range(1, shards)]

    give, right, own, largest = call(
        functools.partial(image_kernel, mids, shards), "image_give",
        nears + aways + kernels,
        [
            like(outs + 8, half * share),
            like(shards * share, 2 * outs, dtype=bf16),
            like(outs, share),
            like(8, share),
        ],
        [pltpu.VMEM((outs, shards * share), f32)],
    )
    received = send_xor(give, 1)
    (keep,) = call(
        functools.partial(image_keep_kernel, mids, share), "image_keep",
        [right] + kernels, [like(outs, half * share)],
    )
    pieces = join(keep, received, [largest], outs + 8)
    pieces = [pieces[0]] + [send_xor(pieces[m], 2 * m) for m in range(mids - 1, 0, -1)]
    keep, give = call(
        functools.partial(theta_kernel, mids, share), "theta",
        [part, own] + pieces, [like(outs, share)] * 2,
    )
    (new_coefficients,) = call(
        final_kernel, "final", [keep, send_xor(give, half), weights], [like(outs, share)]
    )
    return (residual.T, new_coefficients.T)


def solution(mesh):
    return jax.shard_map(
        body,
        mesh=mesh,
        in_specs=(P("dp", None), P("dp", None), P("centre", None), P("centre", None)),
        out_specs=(P("dp", None), P(("centre", "dp"), None)),
        check_vma=False,
    )
```

```python
import functools
import jax
import jax.numpy as jnp
from jax import lax
from jax.experimental import pallas as pl
from jax.experimental.pallas import tpu as pltpu
from jax.sharding import PartitionSpec as P

softening = 0.01
kernel_scale = 0.2
learning_rate = 4.0
f32, bf16 = jnp.float32, jnp.bfloat16
mega = 1024 * 1024


def split(x):
    high = x.astype(bf16)
    return high, (x - high.astype(f32)).astype(bf16)


def dot(left, right):
    return jnp.dot(left, right, preferred_element_type=f32)


def place():
    index, count = lax.axis_index("dp"), lax.axis_size("dp")
    return index, lax.rem(index, 2), lax.rem(index // 2, count // 4), index // (count // 2)


def like(*shape, dtype=f32):
    return jax.ShapeDtypeStruct(shape, dtype)


def call(kernel, name, ins, outs, scratch=(), room=8 * mega, flops=0, space=pltpu.VMEM):
    return pl.pallas_call(
        kernel,
        name=name,
        in_specs=[pl.BlockSpec(memory_space=space)] * len(ins),
        out_specs=[pl.BlockSpec(memory_space=pltpu.VMEM)] * len(outs),
        out_shape=list(outs),
        scratch_shapes=list(scratch),
        compiler_params=pltpu.CompilerParams(vmem_limit_bytes=room),
        cost_estimate=pl.CostEstimate(flops=flops, bytes_accessed=0, transcendentals=0),
    )(*ins)


def points_in(x):
    high, low = split(x.T)
    wide, rest = high.astype(f32), low.astype(f32)
    square = jnp.sum(wide * wide + 2.0 * (wide * rest), axis=0, keepdims=True)
    return (-2.0 * wide).astype(bf16), (-2.0 * rest).astype(bf16), square


def entries(high, low, square, xh, xl, xsq):
    cross = dot(high, xh) + dot(low, xh) + dot(high, xl)
    dist = jnp.maximum(cross + (square + xsq), 0.0) + softening
    return jnp.exp(dist * lax.rsqrt(dist) * (-1.0 / kernel_scale))


def load_kernel(c_hbm, ch_ref, cl_ref, sq_ref, pair_ref, c_ref, sems):
    rows, share = c_ref.shape[0], pair_ref.shape[0] // 2
    index, half = place()[0], lax.axis_size("dp") // 2
    loads = sems.shape[0]
    load = rows // loads
    copies = [
        pltpu.make_async_copy(c_hbm.at[pl.ds(i * load, load)], c_ref.at[pl.ds(i * load, load)], sems.at[i])
        for i in range(loads)
    ]
    for copy in copies:
        copy.start()
    for i, copy in enumerate(copies):
        copy.wait()
        where = slice(i * load, (i + 1) * load)
        high, low = split(c_ref[where, :])
        wide, rest = high.astype(f32), low.astype(f32)
        ch_ref[where, :] = high
        cl_ref[where, :] = low
        sq_ref[where, :] = jnp.sum(wide * wide + 2.0 * (wide * rest), axis=1, keepdims=True)
    for t, at in enumerate((index, lax.rem(index + half, 2 * half))):
        pair_ref[t * share : (t + 1) * share, :] = c_ref[pl.ds(pl.multiple_of(at * share, share), share), :]


def data_kernel(block, x_ref, w_ref, ch_ref, cl_ref, sq_ref, kh_ref, kl_ref, pred_ref, xh_ref, xl_ref):
    rows, outs = ch_ref.shape[0], pred_ref.shape[0]
    xh, xl, xsq = points_in(x_ref[...])
    xh_ref[...] = xh
    xl_ref[...] = xl
    pred = None
    for i in range(rows // block):
        where = slice(i * block, (i + 1) * block)
        tile = entries(ch_ref[where, :], cl_ref[where, :], sq_ref[where, :], xh_ref[...], xl_ref[...], xsq)
        kh, kl = split(tile)
        kh_ref[where, :] = kh
        kl_ref[where, :] = kl
        weights = jnp.concatenate(split(w_ref[:, where]), axis=0)
        part = dot(weights, kh) + dot(weights, kl)
        pred = part if pred is None else pred + part
    pred_ref[...] = pred[:outs, :] + pred[outs:, :]


def centre_kernel(block, *refs):
    x_refs = refs[:-8]
    ch_ref, cl_ref, sq_ref, kh_ref, kl_ref, sum_ref, xh_ref, xl_ref = refs[-8:]
    rows = ch_ref.shape[0]
    at = 0
    for x_ref in x_refs:
        span = slice(at, at + x_ref.shape[0])
        at = span.stop
        xh, xl, xsq = points_in(x_ref[...])
        xh_ref[...] = xh
        xl_ref[...] = xl
        total = None
        for i in range(rows // block):
            where = slice(i * block, (i + 1) * block)
            tile = entries(ch_ref[where, :], cl_ref[where, :], sq_ref[where, :], xh_ref[...], xl_ref[...], xsq)
            kh, kl = split(tile)
            kh_ref[where, span] = kh
            kl_ref[where, span] = kl
            part = jnp.sum(tile.reshape(-1, 8, tile.shape[1]), axis=0)
            total = part if total is None else total + part
        sum_ref[:, span] = total


def share_rows(mids, share, flip, tops=(0, 1)):
    _, core, mid, _ = place()
    for m in range(mids):
        for top in tops:
            block = top * 2 * mids + 2 * (mid ^ m) + (core ^ flip)
            yield pl.ds(pl.multiple_of(block * share, share), share)


def take(ref, where):
    return jnp.concatenate([ref[rows, :] for rows in where], axis=0)


def back(where, parts, right):
    where = list(where)
    product, at = 0.0, 0
    for high, low in parts:
        values = right[at : at + high.shape[1]]
        at += high.shape[1]
        product = product + (dot(take(high, where), values) + dot(take(low, where), values))
    product = product.T
    outs = right.shape[1] // 2
    return product[:outs] + product[outs:]


def grad_kernel(mids, share, *refs):
    t_ref, high_ref, low_ref, out_ref, res_ref, right_ref = refs[-6:]
    total = refs[0][...]
    for ref in refs[1:-6]:
        total = total + ref[...]
    residual = total - t_ref[...]
    res_ref[...] = residual
    right = jnp.concatenate(split(residual.T), axis=1)
    right_ref[...] = right
    out_ref[...] = back(share_rows(mids, share, 1), [(high_ref, low_ref)], right)


def grad_keep_kernel(mids, share, right_ref, high_ref, low_ref, out_ref):
    right = right_ref[...]
    out_ref[...] = back(share_rows(mids, share, 0), [(high_ref, low_ref)], right)


def image_kernel(mids, share, shards, *refs):
    kernels = refs[shards : shards + 4]
    out_ref, right_ref, own_ref, max_ref, image_ref = refs[shards + 4 :]
    outs, size = own_ref.shape[0], 2 * share
    total = refs[0][...]
    for ref in refs[1:shards]:
        total = total + ref[...]
    largest = jnp.max(total[outs : outs + 1], keepdims=True)
    max_ref[...] = jnp.broadcast_to(largest, max_ref.shape)
    out_ref[outs:, :] = jnp.broadcast_to(largest, (8, out_ref.shape[1]))
    image_ref[...] = total[:outs]
    for j in range(shards):
        part = image_ref[:, pl.ds(shard_at(j, shards, size), size)]
        right_ref[j * size : (j + 1) * size, :] = jnp.concatenate(split(part.T), axis=1)
        if j == 0:
            own_ref[...] = part[:, :share]
    where = share_rows(mids, share, 1, [place()[3]])
    out_ref[:outs, :] = back(where, [kernels[:2], kernels[2:]], right_ref[...])


def image_keep_kernel(mids, share, right_ref, *refs):
    where = share_rows(mids, share, 0, [place()[3]])
    refs[-1][...] = back(where, [refs[:2], refs[2:4]], right_ref[...])


def shard_at(j, shards, share):
    return pl.multiple_of(lax.rem(lax.axis_index("centre") + j, shards) * share, share)


def product(mids, share, flip, pieces, kernels):
    where = list(share_rows(mids, share, flip))
    high, low = split(jnp.concatenate([ref[...] for ref in pieces], axis=1))
    left = jnp.concatenate([high, low], axis=0)
    outs = high.shape[0]
    for kh, kl in (kernels[:2], kernels[2:]):
        result = dot(left, take(kh, where)) + dot(left, take(kl, where))
        yield result[:outs] + result[outs:]


def first_kernel(mids, share, *refs):
    own_ref, far_ref = refs[-2:]
    own, far = product(mids, share, 0, refs[:mids], refs[mids : mids + 4])
    own_ref[...] = own
    far_ref[...] = far


def second_kernel(mids, share, shards, *refs):
    own_ref, far_ref, osum, fsum, out_ref = refs[-5:]
    outs, size = own_ref.shape[0], 2 * share
    own, far = product(mids, share, 1, refs[:-9], refs[-9:-5])
    own, far = own + own_ref[...], far + far_ref[...]
    for j in range(shards):
        source, sums, at = (own, osum, 0) if j == 0 else (far, fsum, size * (j - 1))
        where = pl.ds(shard_at(j, shards, size), size)
        out_ref[:outs, where] = source[:, at : at + size]
        row_sums = jnp.sum(sums[:, at : at + size], axis=0, keepdims=True)
        out_ref[outs:, where] = jnp.broadcast_to(row_sums, (8, size))


def pack_kernel(*refs):
    refs[-1][...] = jnp.concatenate([ref[...] for ref in refs[:-1]], axis=1)


def join_kernel(mids, keep_ref, got_ref, *refs):
    outs = keep_ref.shape[0]
    piece_refs = refs[-mids:]
    wide = piece_refs[0].shape[1]
    for m in range(mids):
        columns = slice(m * wide, (m + 1) * wide)
        piece_refs[m][:outs, :] = keep_ref[:, columns] + got_ref[:outs, columns]
    if len(refs) > mids:
        largest = jnp.maximum(refs[0][...], got_ref[outs:, : refs[0].shape[1]])
        for m in range(mids):
            piece_refs[m][outs:, :] = jnp.broadcast_to(largest[:, :1], (8, wide))


def sum_kernel(*refs):
    total = refs[0][...]
    for ref in refs[1:-1]:
        total = total + ref[...]
    refs[-1][...] = total


def final_kernel(mids, whole_ref, own_ref, coeff_ref, *refs):
    pieces, out_ref = refs[:mids], refs[mids]
    outs, share = out_ref.shape
    second = pieces[0][:outs, :]
    largest = pieces[0][outs:, :]
    for ref in pieces[1:]:
        second = second + ref[:outs, :]
        largest = jnp.maximum(largest, ref[outs:, :])
    step = 1.0 / largest[:1, :1]
    index, _, _, top = place()
    gradient = jnp.where(top == 1, whole_ref[:, share:], whole_ref[:, :share])
    theta = 3.0 * step * (gradient - step * own_ref[...]) + (step * step * step) * second
    coefficients = coeff_ref[:, pl.ds(pl.multiple_of(index * share, share), share)]
    out_ref[...] = coefficients - learning_rate * theta


def send_xor(array, mask):
    count = lax.axis_size("dp")
    return lax.ppermute(array, "dp", [(i, i ^ mask) for i in range(count)])


def send_far(array, mask, shift):
    dp, centre = lax.axis_size("dp"), lax.axis_size("centre")
    pairs = [
        (d * centre + c, (d ^ mask) * centre + (c + shift) % centre)
        for d in range(dp)
        for c in range(centre)
    ]
    return lax.ppermute(array, ("dp", "centre"), pairs)


def after(value, *others):
    return lax.optimization_barrier((value, *others))[0]


def body(samples, targets, centres, coefficients):
    count = lax.axis_size("dp")
    shards = lax.axis_size("centre")
    rows, width = centres.shape
    share = rows // count
    points, outs = targets.shape
    half = count // 2
    mids = half // 2
    weights = coefficients.T
    block = min(256, rows)

    loads = min(8, count)
    kept = 4 * rows * width + 512 * rows + 8 * share * width
    ch, cl, square, pair = call(
        load_kernel, "load", [centres],
        [
            like(rows, width, dtype=bf16),
            like(rows, width, dtype=bf16),
            like(rows, 1),
            like(2 * share, width),
        ],
        [pltpu.VMEM((rows, width), f32), pltpu.SemaphoreType.DMA((loads,))],
        room=103 * mega // 2 - kept, space=pltpu.HBM,
    )
    kh, kl, pred = call(
        functools.partial(data_kernel, block), "data", [samples, weights, ch, cl, square],
        [like(rows, points, dtype=bf16), like(rows, points, dtype=bf16), like(outs, points)],
        [pltpu.VMEM((width, points), bf16), pltpu.VMEM((width, points), bf16)],
    )
    got = [send_far(pred, 0, shift) for shift in range(1, shards)]

    def centre_tile(blocks, name):
        size = blocks[0].shape[0]
        columns = size * len(blocks)
        return call(
            functools.partial(centre_kernel, block), name, blocks + [ch, cl, square],
            [like(rows, columns, dtype=bf16), like(rows, columns, dtype=bf16), like(8, columns)],
            [pltpu.VMEM((width, size), bf16), pltpu.VMEM((width, size), bf16)],
            flops=6 * rows * columns * width,
        )

    own_high, own_low, own_sums = centre_tile([after(pair, pred)], "own_tile")
    got[0] = after(got[0], own_high)

    give, residual, right = call(
        functools.partial(grad_kernel, mids, share), "grad_give",
        [pred] + got + [targets.T, kh, kl],
        [like(outs, half * share), like(outs, points), like(points, 2 * outs, dtype=bf16)],
    )
    received = send_xor(give, 1)
    (keep,) = call(
        functools.partial(grad_keep_kernel, mids, share), "grad_keep",
        [right, kh, kl], [like(outs, half * share)],
    )

    def join(keep, received, extra, height):
        return call(
            functools.partial(join_kernel, mids), "join",
            [keep, received] + extra, [like(height, keep.shape[1] // mids)] * mids,
        )

    def total(arrays):
        return call(sum_kernel, "sum", arrays, [like(*arrays[0].shape)])[0]

    def spread(pieces):
        sent = [send_xor(pieces[m], 2 * m) for m in range(mids - 1, 0, -1)]
        return [pieces[0]] + sent[::-1]

    pieces = spread(join(keep, received, [], outs))
    far = [send_far(after(pair, received, keep), 0, -shift) for shift in range(1, shards)]
    part = total(pieces)
    whole = total([part, send_xor(part, half)])
    gathered = spread([whole] * mids)
    far_high, far_low, far_sums = centre_tile([after(f, whole) for f in far], "far_tile")
    kernels = [own_high, own_low, far_high, far_low]
    wide = 2 * share * (shards - 1)
    packed = call(
        pack_kernel, "pack", [after(whole, far_sums)] + gathered[1:], [like(outs, 2 * share * mids)]
    )[0]
    crossed = [send_xor(packed, 1)]
    firsts = call(
        functools.partial(first_kernel, mids, share), "product_first",
        gathered + kernels, [like(outs, 2 * share), like(outs, wide)],
    )
    (image,) = call(
        functools.partial(second_kernel, mids, share, shards), "product_second",
        crossed + kernels + list(firsts) + [own_sums, far_sums],
        [like(outs + 8, 2 * share * shards)],
    )
    images = [image] + [send_far(image, 0, shift) for shift in range(1, shards)]
    give, right, own, largest = call(
        functools.partial(image_kernel, mids, share, shards), "image_give",
        images + kernels,
        [
            like(outs + 8, mids * share),
            like(2 * share * shards, 2 * outs, dtype=bf16),
            like(outs, share),
            like(8, share),
        ],
        [pltpu.VMEM((outs, 2 * share * shards), f32)],
    )
    received = send_xor(give, 1)
    (keep,) = call(
        functools.partial(image_keep_kernel, mids, share), "image_keep",
        [right] + kernels, [like(outs, mids * share)],
    )
    pieces = spread(join(keep, received, [largest], outs + 8))
    (new_coefficients,) = call(
        functools.partial(final_kernel, mids), "final", [whole, own, weights] + pieces, [like(outs, share)]
    )
    return (residual.T, new_coefficients.T)


def solution(mesh):
    return jax.shard_map(
        body,
        mesh=mesh,
        in_specs=(P("dp", None), P("dp", None), P("centre", None), P("centre", None)),
        out_specs=(P("dp", None), P(("centre", "dp"), None)),
        check_vma=False,
    )
```

```python
import functools
import jax
import jax.numpy as jnp
from jax import lax
from jax.experimental import pallas as pl
from jax.experimental.pallas import tpu as pltpu
from jax.sharding import PartitionSpec as P

softening = 0.01
kernel_scale = 0.2
learning_rate = 4.0
f32, bf16 = jnp.float32, jnp.bfloat16
mega = 1024 * 1024


def split(x):
    high = x.astype(bf16)
    return high, (x - high.astype(f32)).astype(bf16)


def dot(left, right):
    return jnp.dot(left, right, preferred_element_type=f32)


def place():
    index, count = lax.axis_index("dp"), lax.axis_size("dp")
    return index, lax.rem(index, 2), lax.rem(index // 2, count // 4), index // (count // 2)


def like(*shape, dtype=f32):
    return jax.ShapeDtypeStruct(shape, dtype)


def call(kernel, name, ins, outs, scratch=(), room=8 * mega, flops=0, far=()):
    return pl.pallas_call(
        kernel,
        name=name,
        in_specs=[pl.BlockSpec(memory_space=pltpu.VMEM)] * len(ins)
        + [pl.BlockSpec(memory_space=pltpu.HBM)] * len(far),
        out_specs=[pl.BlockSpec(memory_space=pltpu.VMEM)] * len(outs),
        out_shape=list(outs),
        scratch_shapes=list(scratch),
        compiler_params=pltpu.CompilerParams(vmem_limit_bytes=room),
        cost_estimate=pl.CostEstimate(flops=flops, bytes_accessed=0, transcendentals=0),
    )(*ins, *far)


def points_in(x):
    high, low = split(x.T)
    wide, rest = high.astype(f32), low.astype(f32)
    square = jnp.sum(wide * wide + 2.0 * (wide * rest), axis=0, keepdims=True)
    return (-2.0 * wide).astype(bf16), (-2.0 * rest).astype(bf16), square


def crossed(high, low, xh, xl):
    return dot(high, xh) + dot(low, xh) + dot(high, xl)


def entries(cross, square, xsq):
    dist = jnp.maximum(cross + (square + xsq), 0.0) + softening
    return jnp.exp(dist * lax.rsqrt(dist) * (-1.0 / kernel_scale))


def staged(count, cross, finish):
    held = cross(0)
    for i in range(count):
        coming = cross(i + 1) if i + 1 < count else None
        finish(i, held)
        held = coming


def rows_in(x, where, high_ref, low_ref, square_ref):
    high, low = split(x)
    wide, rest = high.astype(f32), low.astype(f32)
    high_ref[where, :] = high
    low_ref[where, :] = low
    square_ref[where, :] = jnp.sum(wide * wide + 2.0 * (wide * rest), axis=1, keepdims=True)
    return high, low


def load_kernel(c_hbm, ch_ref, cl_ref, sq_ref, c_ref, sems):
    loads = sems.shape[0]
    load = c_ref.shape[0] // loads
    copies = [
        pltpu.make_async_copy(c_hbm.at[pl.ds(i * load, load)], c_ref.at[pl.ds(i * load, load)], sems.at[i])
        for i in range(loads)
    ]
    for copy in copies:
        copy.start()
    for i, copy in enumerate(copies):
        copy.wait()
        where = slice(i * load, (i + 1) * load)
        rows_in(c_ref[where, :], where, ch_ref, cl_ref, sq_ref)


def first_data_kernel(block, x_ref, ch_ref, cl_ref, sq_ref, c_hbm, *refs):
    kh_ref, kl_ref, xh_ref, xl_ref, xsq_ref, rest_ref, pair_ref, sems = refs
    half, share = rest_ref.shape[0], pair_ref.shape[0] // 2
    index, count = place()[0], lax.axis_size("dp")
    copies = [pltpu.make_async_copy(c_hbm.at[pl.ds(half, half)], rest_ref, sems.at[0])]
    for t, at in enumerate((index, lax.rem(index + count // 2, count))):
        where = pl.ds(pl.multiple_of(at * share, share), share)
        copies.append(
            pltpu.make_async_copy(c_hbm.at[where], pair_ref.at[pl.ds(t * share, share)], sems.at[1 + t])
        )
    for copy in copies:
        copy.start()
    xh, xl, xsq = points_in(x_ref[...])
    xh_ref[...] = xh
    xl_ref[...] = xl
    xsq_ref[...] = xsq

    def cross(i):
        where = slice(i * block, (i + 1) * block)
        return crossed(ch_ref[where, :], cl_ref[where, :], xh_ref[...], xl_ref[...])

    def finish(i, value):
        where = slice(i * block, (i + 1) * block)
        kh, kl = split(entries(value, sq_ref[where, :], xsq))
        kh_ref[where, :] = kh
        kl_ref[where, :] = kl

    staged(half // block, cross, finish)
    for copy in copies:
        copy.wait()


def second_data_kernel(block, w_ref, rest_ref, xh_ref, xl_ref, xsq_ref, first_h, first_l, *refs):
    ch_ref, cl_ref, sq_ref, kh_ref, kl_ref, pred_ref = refs
    half, outs = rest_ref.shape[0], pred_ref.shape[0]

    def cross(i):
        where = slice(i * block, (i + 1) * block)
        high, low = rows_in(rest_ref[where, :], where, ch_ref, cl_ref, sq_ref)
        return crossed(high, low, xh_ref[...], xl_ref[...])

    def finish(i, value):
        where = slice(i * block, (i + 1) * block)
        kh, kl = split(entries(value, sq_ref[where, :], xsq_ref[...]))
        kh_ref[where, :] = kh
        kl_ref[where, :] = kl

    staged(half // block, cross, finish)
    weights = jnp.concatenate(split(w_ref[...]), axis=0)
    pred = dot(weights[:, :half], first_h[...]) + dot(weights[:, :half], first_l[...])
    pred = pred + (dot(weights[:, half:], kh_ref[...]) + dot(weights[:, half:], kl_ref[...]))
    pred_ref[...] = pred[:outs, :] + pred[outs:, :]


def centre_kernel(block, *refs):
    x_refs, centres = refs[:-11], (refs[-11:-8], refs[-8:-5])
    kh_ref, kl_ref, sum_ref, xh_ref, xl_ref = refs[-5:]
    half = centres[0][0].shape[0]
    at = 0
    for x_ref in x_refs:
        span = slice(at, at + x_ref.shape[0])
        at = span.stop
        xh, xl, xsq = points_in(x_ref[...])
        xh_ref[...] = xh
        xl_ref[...] = xl
        sums = []

        def cross(i):
            high, low, _ = centres[i * block // half]
            where = slice(i * block % half, i * block % half + block)
            return crossed(high[where, :], low[where, :], xh_ref[...], xl_ref[...])

        def finish(i, value):
            square = centres[i * block // half][2]
            tile = entries(value, square[i * block % half : i * block % half + block, :], xsq)
            where = slice(i * block, (i + 1) * block)
            kh, kl = split(tile)
            kh_ref[where, span] = kh
            kl_ref[where, span] = kl
            sums.append(jnp.sum(tile.reshape(-1, 8, tile.shape[1]), axis=0))

        staged(2 * half // block, cross, finish)
        sum_ref[:, span] = sum(sums[1:], sums[0])


def share_blocks(mids, flip, tops=(0, 1)):
    _, core, mid, _ = place()
    return [(top, 2 * (mid ^ m) + (core ^ flip)) for m in range(mids) for top in tops]


def take(ref, where, share):
    rows = []
    for top, block in where:
        source = ref[top] if isinstance(ref, tuple) else ref
        at = block if isinstance(ref, tuple) else top * (source.shape[0] // share // 2) + block
        rows.append(source[pl.ds(pl.multiple_of(at * share, share), share), :])
    return jnp.concatenate(rows, axis=0)


def back(where, share, parts, right):
    product, at = 0.0, 0
    for high, low in parts:
        high, low = take(high, where, share), take(low, where, share)
        values = right[at : at + high.shape[1]]
        at += high.shape[1]
        product = product + (dot(high, values) + dot(low, values))
    product = product.T
    outs = right.shape[1] // 2
    return product[:outs] + product[outs:]


def grad_kernel(mids, share, *refs):
    t_ref, kernels, (out_ref, res_ref, right_ref) = refs[-8], refs[-7:-3], refs[-3:]
    total = refs[0][...]
    for ref in refs[1:-8]:
        total = total + ref[...]
    residual = total - t_ref[...]
    res_ref[...] = residual
    right = jnp.concatenate(split(residual.T), axis=1)
    right_ref[...] = right
    out_ref[...] = back(share_blocks(mids, 1), share, [(kernels[:2], kernels[2:])], right)


def grad_keep_kernel(mids, share, right_ref, *refs):
    out_ref = refs[4]
    out_ref[...] = back(share_blocks(mids, 0), share, [(refs[:2], refs[2:4])], right_ref[...])


def image_kernel(mids, share, shards, *refs):
    kernels = refs[shards : shards + 4]
    out_ref, right_ref, own_ref, max_ref, image_ref = refs[shards + 4 :]
    outs, size = own_ref.shape[0], 2 * share
    total = refs[0][...]
    for ref in refs[1:shards]:
        total = total + ref[...]
    largest = jnp.max(total[outs : outs + 1], keepdims=True)
    max_ref[...] = jnp.broadcast_to(largest, max_ref.shape)
    out_ref[outs:, :] = jnp.broadcast_to(largest, (8, out_ref.shape[1]))
    image_ref[...] = total[:outs]
    for j in range(shards):
        part = image_ref[:, pl.ds(shard_at(j, shards, size), size)]
        right_ref[j * size : (j + 1) * size, :] = jnp.concatenate(split(part.T), axis=1)
        if j == 0:
            own_ref[...] = part[:, :share]
    where = share_blocks(mids, 1, [place()[3]])
    out_ref[:outs, :] = back(where, share, [kernels[:2], kernels[2:]], right_ref[...])


def image_keep_kernel(mids, share, right_ref, *refs):
    where = share_blocks(mids, 0, [place()[3]])
    refs[-1][...] = back(where, share, [refs[:2], refs[2:4]], right_ref[...])


def shard_at(j, shards, share):
    return pl.multiple_of(lax.rem(lax.axis_index("centre") + j, shards) * share, share)


def product(mids, share, flip, pieces, kernels):
    where = share_blocks(mids, flip)
    high, low = split(jnp.concatenate([ref[...] for ref in pieces], axis=1))
    left = jnp.concatenate([high, low], axis=0)
    outs = high.shape[0]
    for kh, kl in (kernels[:2], kernels[2:]):
        result = dot(left, take(kh, where, share)) + dot(left, take(kl, where, share))
        yield result[:outs] + result[outs:]


def first_kernel(mids, share, *refs):
    own_ref, far_ref = refs[-2:]
    own, far = product(mids, share, 0, refs[:mids], refs[mids : mids + 4])
    own_ref[...] = own
    far_ref[...] = far


def second_kernel(mids, share, shards, *refs):
    own_ref, far_ref, osum, fsum, out_ref = refs[-5:]
    outs, size = own_ref.shape[0], 2 * share
    own, far = product(mids, share, 1, refs[:-9], refs[-9:-5])
    own, far = own + own_ref[...], far + far_ref[...]
    for j in range(shards):
        source, sums, at = (own, osum, 0) if j == 0 else (far, fsum, size * (j - 1))
        where = pl.ds(shard_at(j, shards, size), size)
        out_ref[:outs, where] = source[:, at : at + size]
        row_sums = jnp.sum(sums[:, at : at + size], axis=0, keepdims=True)
        out_ref[outs:, where] = jnp.broadcast_to(row_sums, (8, size))


def pack_kernel(*refs):
    refs[-1][...] = jnp.concatenate([ref[...] for ref in refs[:-1]], axis=1)


def join_kernel(mids, keep_ref, got_ref, *refs):
    outs = keep_ref.shape[0]
    piece_refs = refs[-mids:]
    wide = piece_refs[0].shape[1]
    for m in range(mids):
        columns = slice(m * wide, (m + 1) * wide)
        piece_refs[m][:outs, :] = keep_ref[:, columns] + got_ref[:outs, columns]
    if len(refs) > mids:
        largest = jnp.maximum(refs[0][...], got_ref[outs:, : refs[0].shape[1]])
        for m in range(mids):
            piece_refs[m][outs:, :] = jnp.broadcast_to(largest[:, :1], (8, wide))


def sum_kernel(*refs):
    total = refs[0][...]
    for ref in refs[1:-1]:
        total = total + ref[...]
    refs[-1][...] = total


def final_kernel(mids, whole_ref, own_ref, coeff_ref, *refs):
    pieces, out_ref = refs[:mids], refs[mids]
    outs, share = out_ref.shape
    second = pieces[0][:outs, :]
    largest = pieces[0][outs:, :]
    for ref in pieces[1:]:
        second = second + ref[:outs, :]
        largest = jnp.maximum(largest, ref[outs:, :])
    step = 1.0 / largest[:1, :1]
    index, _, _, top = place()
    gradient = jnp.where(top == 1, whole_ref[:, share:], whole_ref[:, :share])
    theta = 3.0 * step * (gradient - step * own_ref[...]) + (step * step * step) * second
    coefficients = coeff_ref[:, pl.ds(pl.multiple_of(index * share, share), share)]
    out_ref[...] = coefficients - learning_rate * theta


def send_xor(array, mask):
    count = lax.axis_size("dp")
    return lax.ppermute(array, "dp", [(i, i ^ mask) for i in range(count)])


def send_far(array, mask, shift):
    dp, centre = lax.axis_size("dp"), lax.axis_size("centre")
    pairs = [
        (d * centre + c, (d ^ mask) * centre + (c + shift) % centre)
        for d in range(dp)
        for c in range(centre)
    ]
    return lax.ppermute(array, ("dp", "centre"), pairs)


def after(value, *others):
    return lax.optimization_barrier((value, *others))[0]


def body(samples, targets, centres, coefficients):
    count = lax.axis_size("dp")
    shards = lax.axis_size("centre")
    rows, width = centres.shape
    share = rows // count
    points, outs = targets.shape
    half = count // 2
    mids = half // 2
    weights = coefficients.T
    block = min(256, rows)

    part = rows // 2
    loads = min(4, count)
    kept = 2 * part * width * 2 + 512 * part
    loaded = call(
        load_kernel, "load", [], [like(part, width, dtype=bf16), like(part, width, dtype=bf16), like(part, 1)],
        [pltpu.VMEM((part, width), f32), pltpu.SemaphoreType.DMA((loads,))],
        room=53 * mega - kept - 4 * points * width, far=[centres],
    )
    kept = 2 * kept + 8 * points * width + 4 * part * (points + width) + 8 * share * width
    kh0, kl0, xh, xl, xsq, rest, pair = call(
        functools.partial(first_data_kernel, block // 2), "data_first", [samples] + list(loaded),
        [
            like(part, points, dtype=bf16),
            like(part, points, dtype=bf16),
            like(width, points, dtype=bf16),
            like(width, points, dtype=bf16),
            like(1, points),
            like(part, width),
            like(2 * share, width),
        ],
        [pltpu.SemaphoreType.DMA((3,))],
        room=107 * mega // 2 - kept, far=[centres],
    )
    ch, cl, square, kh1, kl1, pred = call(
        functools.partial(second_data_kernel, block // 2), "data_second",
        [weights, rest, xh, xl, xsq, kh0, kl0],
        [
            like(part, width, dtype=bf16),
            like(part, width, dtype=bf16),
            like(part, 1),
            like(part, points, dtype=bf16),
            like(part, points, dtype=bf16),
            like(outs, points),
        ],
    )
    halves = list(loaded) + [ch, cl, square]
    kernel = [kh0, kh1, kl0, kl1]
    got = [send_far(pred, 0, shift) for shift in range(1, shards)]

    def centre_tile(blocks, name):
        size = blocks[0].shape[0]
        columns = size * len(blocks)
        return call(
            functools.partial(centre_kernel, block // 2), name, blocks + halves,
            [like(rows, columns, dtype=bf16), like(rows, columns, dtype=bf16), like(8, columns)],
            [pltpu.VMEM((width, size), bf16), pltpu.VMEM((width, size), bf16)],
            flops=6 * rows * columns * width,
        )

    own_high, own_low, own_sums = centre_tile([after(pair, pred)], "own_tile")
    got[0] = after(got[0], own_high)

    give, residual, right = call(
        functools.partial(grad_kernel, mids, share), "grad_give",
        [pred] + got + [targets.T] + kernel,
        [like(outs, half * share), like(outs, points), like(points, 2 * outs, dtype=bf16)],
    )
    received = send_xor(give, 1)
    (keep,) = call(
        functools.partial(grad_keep_kernel, mids, share), "grad_keep",
        [right] + kernel, [like(outs, half * share)],
    )

    def join(keep, received, extra, height):
        return call(
            functools.partial(join_kernel, mids), "join",
            [keep, received] + extra, [like(height, keep.shape[1] // mids)] * mids,
        )

    def total(arrays):
        return call(sum_kernel, "sum", arrays, [like(*arrays[0].shape)])[0]

    def spread(pieces):
        sent = [send_xor(pieces[m], 2 * m) for m in range(mids - 1, 0, -1)]
        return [pieces[0]] + sent[::-1]

    pieces = spread(join(keep, received, [], outs))
    far = [send_far(after(pair, received, keep), 0, -shift) for shift in range(1, shards)]
    part = total(pieces)
    whole = total([part, send_xor(part, half)])
    gathered = spread([whole] * mids)
    far_high, far_low, far_sums = centre_tile([after(f, whole) for f in far], "far_tile")
    kernels = [own_high, own_low, far_high, far_low]
    wide = 2 * share * (shards - 1)
    packed = call(
        pack_kernel, "pack", [after(whole, far_sums)] + gathered[1:], [like(outs, 2 * share * mids)]
    )[0]
    swapped = [send_xor(packed, 1)]
    firsts = call(
        functools.partial(first_kernel, mids, share), "product_first",
        gathered + kernels, [like(outs, 2 * share), like(outs, wide)],
    )
    (image,) = call(
        functools.partial(second_kernel, mids, share, shards), "product_second",
        swapped + kernels + list(firsts) + [own_sums, far_sums],
        [like(outs + 8, 2 * share * shards)],
    )
    images = [image] + [send_far(image, 0, shift) for shift in range(1, shards)]
    give, right, own, largest = call(
        functools.partial(image_kernel, mids, share, shards), "image_give",
        images + kernels,
        [
            like(outs + 8, mids * share),
            like(2 * share * shards, 2 * outs, dtype=bf16),
            like(outs, share),
            like(8, share),
        ],
        [pltpu.VMEM((outs, 2 * share * shards), f32)],
    )
    received = send_xor(give, 1)
    (keep,) = call(
        functools.partial(image_keep_kernel, mids, share), "image_keep",
        [right] + kernels, [like(outs, mids * share)],
    )
    pieces = spread(join(keep, received, [largest], outs + 8))
    (new_coefficients,) = call(
        functools.partial(final_kernel, mids), "final", [whole, own, weights] + pieces, [like(outs, share)]
    )
    return (residual.T, new_coefficients.T)


def solution(mesh):
    return jax.shard_map(
        body,
        mesh=mesh,
        in_specs=(P("dp", None), P("dp", None), P("centre", None), P("centre", None)),
        out_specs=(P("dp", None), P(("centre", "dp"), None)),
        check_vma=False,
    )
```

```python
import functools
import jax
import jax.numpy as jnp
from jax import lax
from jax.experimental import pallas as pl
from jax.experimental.pallas import tpu as pltpu
from jax.sharding import PartitionSpec as P

softening = 0.01
kernel_scale = 0.2
learning_rate = 4.0
f32, bf16 = jnp.float32, jnp.bfloat16
mega = 1024 * 1024


def split(x):
    high = x.astype(bf16)
    return high, (x - high.astype(f32)).astype(bf16)


def dot(left, right):
    return jnp.dot(left, right, preferred_element_type=f32)


def dot_rows(left, right):
    return lax.dot_general(left, right, (((1,), (1,)), ((), ())), preferred_element_type=f32)


def place():
    index, count = lax.axis_index("dp"), lax.axis_size("dp")
    return index, lax.rem(index, 2), lax.rem(index // 2, count // 4), index // (count // 2)


def like(*shape, dtype=f32):
    return jax.ShapeDtypeStruct(shape, dtype)


def call(kernel, name, ins, outs, scratch=(), room=8 * mega, flops=0, far=()):
    return pl.pallas_call(
        kernel,
        name=name,
        in_specs=[pl.BlockSpec(memory_space=pltpu.VMEM)] * len(ins)
        + [pl.BlockSpec(memory_space=pltpu.HBM)] * len(far),
        out_specs=[pl.BlockSpec(memory_space=pltpu.VMEM)] * len(outs),
        out_shape=list(outs),
        scratch_shapes=list(scratch),
        compiler_params=pltpu.CompilerParams(vmem_limit_bytes=room),
        cost_estimate=pl.CostEstimate(flops=flops, bytes_accessed=0, transcendentals=0),
    )(*ins, *far)


def points_in(x):
    high, low = split(x.T)
    wide, rest = high.astype(f32), low.astype(f32)
    square = jnp.sum(wide * wide + 2.0 * (wide * rest), axis=0, keepdims=True)
    return (-2.0 * wide).astype(bf16), (-2.0 * rest).astype(bf16), square


def crossed(high, low, xh, xl):
    return dot(high, xh) + dot(low, xh) + dot(high, xl)


def entries(cross, square, xsq):
    dist = jnp.maximum(cross + (square + xsq), 0.0) + softening
    return jnp.exp(dist * lax.rsqrt(dist) * (-1.0 / kernel_scale))


def staged(count, cross, finish):
    held = cross(0)
    for i in range(count):
        coming = cross(i + 1) if i + 1 < count else None
        finish(i, held)
        held = coming


def rows_in(x, where, high_ref, low_ref, square_ref):
    high, low = split(x)
    wide, rest = high.astype(f32), low.astype(f32)
    high_ref[where, :] = high
    low_ref[where, :] = low
    square_ref[where, :] = jnp.sum(wide * wide + 2.0 * (wide * rest), axis=1, keepdims=True)
    return high, low


def own_block(ref, share):
    at = lax.rem(place()[0], ref.shape[0] // share) * share
    return ref[pl.ds(pl.multiple_of(at, share), share), :]


def load_kernel(c_hbm, ch_ref, cl_ref, sq_ref, first_ref, c_ref, sems):
    loads = sems.shape[0]
    load = c_ref.shape[0] // loads
    copies = [
        pltpu.make_async_copy(c_hbm.at[pl.ds(i * load, load)], c_ref.at[pl.ds(i * load, load)], sems.at[i])
        for i in range(loads)
    ]
    for copy in copies:
        copy.start()
    for i, copy in enumerate(copies):
        copy.wait()
        where = slice(i * load, (i + 1) * load)
        rows_in(c_ref[where, :], where, ch_ref, cl_ref, sq_ref)
    first_ref[...] = own_block(c_ref, first_ref.shape[0])


def first_data_kernel(block, x_ref, ch_ref, cl_ref, sq_ref, c_hbm, *refs):
    kh_ref, kl_ref, xh_ref, xl_ref, xsq_ref, rest_ref, sem = refs
    half = rest_ref.shape[0]
    copy = pltpu.make_async_copy(c_hbm.at[pl.ds(half, half)], rest_ref, sem)
    copy.start()
    xh, xl, xsq = points_in(x_ref[...])
    xh_ref[...] = xh
    xl_ref[...] = xl
    xsq_ref[...] = xsq

    def cross(i):
        where = slice(i * block, (i + 1) * block)
        return crossed(ch_ref[where, :], cl_ref[where, :], xh_ref[...], xl_ref[...])

    def finish(i, value):
        where = slice(i * block, (i + 1) * block)
        kh, kl = split(entries(value, sq_ref[where, :], xsq))
        kh_ref[where, :] = kh
        kl_ref[where, :] = kl

    staged(half // block, cross, finish)
    copy.wait()


def second_data_kernel(block, w_ref, rest_ref, pair0_ref, xh_ref, xl_ref, xsq_ref, first_h, first_l, *refs):
    ch_ref, cl_ref, sq_ref, kh_ref, kl_ref, pred_ref, pair_ref = refs
    half, outs, share = rest_ref.shape[0], pred_ref.shape[0], pair0_ref.shape[0]
    pair_ref[:share, :] = pair0_ref[...]
    pair_ref[share:, :] = own_block(rest_ref, share)

    def cross(i):
        where = slice(i * block, (i + 1) * block)
        high, low = rows_in(rest_ref[where, :], where, ch_ref, cl_ref, sq_ref)
        return crossed(high, low, xh_ref[...], xl_ref[...])

    def finish(i, value):
        where = slice(i * block, (i + 1) * block)
        kh, kl = split(entries(value, sq_ref[where, :], xsq_ref[...]))
        kh_ref[where, :] = kh
        kl_ref[where, :] = kl

    staged(half // block, cross, finish)
    weights = jnp.concatenate(split(w_ref[...]), axis=0)
    pred = dot(weights[:, :half], first_h[...]) + dot(weights[:, :half], first_l[...])
    pred = pred + (dot(weights[:, half:], kh_ref[...]) + dot(weights[:, half:], kl_ref[...]))
    pred_ref[...] = pred[:outs, :] + pred[outs:, :]


def centre_kernel(block, *refs):
    x_refs, centres = refs[:-11], (refs[-11:-8], refs[-8:-5])
    kh_ref, kl_ref, sum_ref, xh_ref, xl_ref = refs[-5:]
    half = centres[0][0].shape[0]
    at = 0
    for x_ref in x_refs:
        span = slice(at, at + x_ref.shape[0])
        at = span.stop
        xh, xl, xsq = points_in(x_ref[...])
        xh_ref[...] = xh
        xl_ref[...] = xl
        sums = []

        def cross(i):
            high, low, _ = centres[i * block // half]
            where = slice(i * block % half, i * block % half + block)
            return crossed(high[where, :], low[where, :], xh_ref[...], xl_ref[...])

        def finish(i, value):
            square = centres[i * block // half][2]
            tile = entries(value, square[i * block % half : i * block % half + block, :], xsq)
            where = slice(i * block, (i + 1) * block)
            kh, kl = split(tile)
            kh_ref[where, span] = kh
            kl_ref[where, span] = kl
            sums.append(jnp.sum(tile.reshape(-1, 8, tile.shape[1]), axis=0))

        staged(2 * half // block, cross, finish)
        sum_ref[:, span] = sum(sums[1:], sums[0])


def share_blocks(mids, flip, tops=(0, 1)):
    _, core, mid, _ = place()
    return [(top, 2 * (mid ^ m) + (core ^ flip)) for m in range(mids) for top in tops]


def take(ref, spot, share):
    top, block = spot
    source = ref[top] if isinstance(ref, tuple) else ref
    at = block if isinstance(ref, tuple) else top * (source.shape[0] // share // 2) + block
    return source[pl.ds(pl.multiple_of(at * share, share), share), :]


def back(where, share, parts, left, out_ref):
    outs = left.shape[0] // 2
    for j, spot in enumerate(where):
        product, at = 0.0, 0
        for high, low in parts:
            high, low = take(high, spot, share), take(low, spot, share)
            values = left[:, at : at + high.shape[1]]
            at += high.shape[1]
            product = product + (dot_rows(values, high) + dot_rows(values, low))
        out_ref[:outs, j * share : (j + 1) * share] = product[:outs] + product[outs:]


def grad_kernel(mids, share, *refs):
    t_ref, kernels, (out_ref, res_ref, left_ref) = refs[-8], refs[-7:-3], refs[-3:]
    total = refs[0][...]
    for ref in refs[1:-8]:
        total = total + ref[...]
    residual = total - t_ref[...]
    res_ref[...] = residual
    left = jnp.concatenate(split(residual), axis=0)
    left_ref[...] = left
    back(share_blocks(mids, 1), share, [(kernels[:2], kernels[2:])], left, out_ref)


def grad_keep_kernel(mids, share, left_ref, *refs):
    back(share_blocks(mids, 0), share, [(refs[:2], refs[2:4])], left_ref[...], refs[4])


def image_kernel(mids, share, shards, *refs):
    kernels = refs[shards : shards + 4]
    out_ref, left_ref, own_ref, max_ref, image_ref = refs[shards + 4 :]
    outs, size = own_ref.shape[0], 2 * share
    total = refs[0][...]
    for ref in refs[1:shards]:
        total = total + ref[...]
    largest = jnp.max(total[outs : outs + 1], keepdims=True)
    max_ref[...] = jnp.broadcast_to(largest, max_ref.shape)
    out_ref[outs:, :] = jnp.broadcast_to(largest, (8, out_ref.shape[1]))
    image_ref[...] = total[:outs]
    for j in range(shards):
        part = image_ref[:, pl.ds(shard_at(j, shards, size), size)]
        left_ref[:, j * size : (j + 1) * size] = jnp.concatenate(split(part), axis=0)
        if j == 0:
            own_ref[...] = jnp.where(place()[3] == 1, part[:, share:], part[:, :share])
    where = share_blocks(mids, 1, [place()[3]])
    back(where, share, [kernels[:2], kernels[2:]], left_ref[...], out_ref)


def image_keep_kernel(mids, share, left_ref, *refs):
    where = share_blocks(mids, 0, [place()[3]])
    back(where, share, [refs[:2], refs[2:4]], left_ref[...], refs[-1])


def shard_at(j, shards, share):
    return pl.multiple_of(lax.rem(lax.axis_index("centre") + j, shards) * share, share)


def rows_of(ref, where, share):
    return jnp.concatenate([take(ref, spot, share) for spot in where], axis=0)


def product(mids, share, flip, pieces, kernels):
    where = share_blocks(mids, flip)
    high, low = split(jnp.concatenate([ref[...] for ref in pieces], axis=1))
    left = jnp.concatenate([high, low], axis=0)
    outs = high.shape[0]
    for kh, kl in (kernels[:2], kernels[2:]):
        result = dot(left, rows_of(kh, where, share)) + dot(left, rows_of(kl, where, share))
        yield result[:outs] + result[outs:]


def first_kernel(mids, share, *refs):
    own_ref, far_ref = refs[-2:]
    own, far = product(mids, share, 0, refs[:mids], refs[mids : mids + 4])
    own_ref[...] = own
    far_ref[...] = far


def second_kernel(mids, share, shards, *refs):
    own_ref, far_ref, osum, fsum, out_ref = refs[-5:]
    outs, size = own_ref.shape[0], 2 * share
    own, far = product(mids, share, 1, refs[:-9], refs[-9:-5])
    own, far = own + own_ref[...], far + far_ref[...]
    for j in range(shards):
        source, sums, at = (own, osum, 0) if j == 0 else (far, fsum, size * (j - 1))
        where = pl.ds(shard_at(j, shards, size), size)
        out_ref[:outs, where] = source[:, at : at + size]
        row_sums = jnp.sum(sums[:, at : at + size], axis=0, keepdims=True)
        out_ref[outs:, where] = jnp.broadcast_to(row_sums, (8, size))


def pack_kernel(*refs):
    refs[-1][...] = jnp.concatenate([ref[...] for ref in refs[:-1]], axis=1)


def join_kernel(mids, keep_ref, got_ref, *refs):
    outs = keep_ref.shape[0]
    piece_refs = refs[-mids:]
    wide = piece_refs[0].shape[1]
    for m in range(mids):
        columns = slice(m * wide, (m + 1) * wide)
        piece_refs[m][:outs, :] = keep_ref[:, columns] + got_ref[:outs, columns]
    if len(refs) > mids:
        largest = jnp.maximum(refs[0][...], got_ref[outs:, : refs[0].shape[1]])
        for m in range(mids):
            piece_refs[m][outs:, :] = jnp.broadcast_to(largest[:, :1], (8, wide))


def sum_kernel(*refs):
    total = refs[0][...]
    for ref in refs[1:-1]:
        total = total + ref[...]
    refs[-1][...] = total


def final_kernel(mids, whole_ref, own_ref, coeff_ref, *refs):
    pieces, out_ref = refs[:mids], refs[mids]
    outs, share = out_ref.shape
    second = pieces[0][:outs, :]
    largest = pieces[0][outs:, :]
    for ref in pieces[1:]:
        second = second + ref[:outs, :]
        largest = jnp.maximum(largest, ref[outs:, :])
    step = 1.0 / largest[:1, :1]
    index, _, _, top = place()
    gradient = jnp.where(top == 1, whole_ref[:, share:], whole_ref[:, :share])
    theta = 3.0 * step * (gradient - step * own_ref[...]) + (step * step * step) * second
    coefficients = coeff_ref[:, pl.ds(pl.multiple_of(index * share, share), share)]
    out_ref[...] = coefficients - learning_rate * theta


def send_xor(array, mask):
    count = lax.axis_size("dp")
    return lax.ppermute(array, "dp", [(i, i ^ mask) for i in range(count)])


def send_far(array, mask, shift):
    dp, centre = lax.axis_size("dp"), lax.axis_size("centre")
    pairs = [
        (d * centre + c, (d ^ mask) * centre + (c + shift) % centre)
        for d in range(dp)
        for c in range(centre)
    ]
    return lax.ppermute(array, ("dp", "centre"), pairs)


def after(value, *others):
    return lax.optimization_barrier((value, *others))[0]


def body(samples, targets, centres, coefficients):
    count = lax.axis_size("dp")
    shards = lax.axis_size("centre")
    rows, width = centres.shape
    share = rows // count
    points, outs = targets.shape
    half = count // 2
    mids = half // 2
    weights = coefficients.T
    block = min(256, rows)

    part = rows // 2
    loads = min(4, count)
    kept = 4 * part * width + 512 * part + 4 * share * width
    *loaded, first = call(
        load_kernel, "load", [],
        [
            like(part, width, dtype=bf16),
            like(part, width, dtype=bf16),
            like(part, 1),
            like(share, width),
        ],
        [pltpu.VMEM((part, width), f32), pltpu.SemaphoreType.DMA((loads,))],
        room=53 * mega - kept - 4 * points * width, far=[centres],
    )
    kept = 2 * kept + 8 * points * width + 4 * part * (points + width)
    kh0, kl0, xh, xl, xsq, rest = call(
        functools.partial(first_data_kernel, block // 2), "data_first", [samples] + loaded,
        [
            like(part, points, dtype=bf16),
            like(part, points, dtype=bf16),
            like(width, points, dtype=bf16),
            like(width, points, dtype=bf16),
            like(1, points),
            like(part, width),
        ],
        [pltpu.SemaphoreType.DMA],
        room=107 * mega // 2 - kept, far=[centres],
    )
    ch, cl, square, kh1, kl1, pred, pair = call(
        functools.partial(second_data_kernel, block // 2), "data_second",
        [weights, rest, first, xh, xl, xsq, kh0, kl0],
        [
            like(part, width, dtype=bf16),
            like(part, width, dtype=bf16),
            like(part, 1),
            like(part, points, dtype=bf16),
            like(part, points, dtype=bf16),
            like(outs, points),
            like(2 * share, width),
        ],
    )
    halves = loaded + [ch, cl, square]
    kernel = [kh0, kh1, kl0, kl1]
    got = [send_far(pred, 0, shift) for shift in range(1, shards)]
    far = [send_far(pair, 0, -shift) for shift in range(1, shards)]

    def centre_tile(blocks, name):
        size = blocks[0].shape[0]
        columns = size * len(blocks)
        return call(
            functools.partial(centre_kernel, block // 2), name, blocks + halves,
            [like(rows, columns, dtype=bf16), like(rows, columns, dtype=bf16), like(8, columns)],
            [pltpu.VMEM((width, size), bf16), pltpu.VMEM((width, size), bf16)],
            flops=6 * rows * columns * width,
        )

    own_high, own_low, own_sums = centre_tile([after(pair, pred)], "own_tile")
    got[0] = after(got[0], own_high)

    give, residual, left = call(
        functools.partial(grad_kernel, mids, share), "grad_give",
        [pred] + got + [targets.T] + kernel,
        [like(outs, half * share), like(outs, points), like(2 * outs, points, dtype=bf16)],
    )
    received = send_xor(give, 1)
    (keep,) = call(
        functools.partial(grad_keep_kernel, mids, share), "grad_keep",
        [left] + kernel, [like(outs, half * share)],
    )

    def join(keep, received, extra, height):
        return call(
            functools.partial(join_kernel, mids), "join",
            [keep, received] + extra, [like(height, keep.shape[1] // mids)] * mids,
        )

    def total(arrays):
        return call(sum_kernel, "sum", arrays, [like(*arrays[0].shape)])[0]

    def spread(pieces):
        sent = [send_xor(pieces[m], 2 * m) for m in range(mids - 1, 0, -1)]
        return [pieces[0]] + sent[::-1]

    part = total(spread(join(keep, received, [], outs)))
    whole = total([part, send_xor(part, half)])
    gathered = spread([whole] * mids)
    far_high, far_low, far_sums = centre_tile([after(f, whole) for f in far], "far_tile")
    kernels = [own_high, own_low, far_high, far_low]
    wide = 2 * share * (shards - 1)
    packed = call(
        pack_kernel, "pack", [after(whole, far_sums)] + gathered[1:], [like(outs, 2 * share * mids)]
    )[0]
    swapped = [send_xor(packed, 1)]
    firsts = call(
        functools.partial(first_kernel, mids, share), "product_first",
        gathered + kernels, [like(outs, 2 * share), like(outs, wide)],
    )
    (image,) = call(
        functools.partial(second_kernel, mids, share, shards), "product_second",
        swapped + kernels + list(firsts) + [own_sums, far_sums],
        [like(outs + 8, 2 * share * shards)],
    )
    images = [image] + [send_far(image, 0, shift) for shift in range(1, shards)]
    give, left, own, largest = call(
        functools.partial(image_kernel, mids, share, shards), "image_give",
        images + kernels,
        [
            like(outs + 8, mids * share),
            like(2 * outs, 2 * share * shards, dtype=bf16),
            like(outs, share),
            like(8, share),
        ],
        [pltpu.VMEM((outs, 2 * share * shards), f32)],
    )
    received = send_xor(give, 1)
    (keep,) = call(
        functools.partial(image_keep_kernel, mids, share), "image_keep",
        [left] + kernels, [like(outs, mids * share)],
    )
    pieces = spread(join(keep, received, [largest], outs + 8))
    (new_coefficients,) = call(
        functools.partial(final_kernel, mids), "final", [whole, own, weights] + pieces, [like(outs, share)]
    )
    return (residual.T, new_coefficients.T)


def solution(mesh):
    return jax.shard_map(
        body,
        mesh=mesh,
        in_specs=(P("dp", None), P("dp", None), P("centre", None), P("centre", None)),
        out_specs=(P("dp", None), P(("centre", "dp"), None)),
        check_vma=False,
    )
```

```python
import functools
import jax
import jax.numpy as jnp
from jax import lax
from jax.experimental import pallas as pl
from jax.experimental.pallas import tpu as pltpu
from jax.sharding import PartitionSpec as P

softening = 0.01
kernel_scale = 0.2
learning_rate = 4.0
f32, bf16 = jnp.float32, jnp.bfloat16
mega = 1024 * 1024


def split(x):
    high = x.astype(bf16)
    return high, (x - high.astype(f32)).astype(bf16)


def dot(left, right):
    return jnp.dot(left, right, preferred_element_type=f32)


def dot_rows(left, right):
    return lax.dot_general(left, right, (((1,), (1,)), ((), ())), preferred_element_type=f32)


def place():
    index, count = lax.axis_index("dp"), lax.axis_size("dp")
    return index, lax.rem(index, 2), lax.rem(index // 2, count // 4), index // (count // 2)


def like(*shape, dtype=f32):
    return jax.ShapeDtypeStruct(shape, dtype)


def call(kernel, name, ins, outs, scratch=(), room=8 * mega, flops=0, far=()):
    return pl.pallas_call(
        kernel,
        name=name,
        in_specs=[pl.BlockSpec(memory_space=pltpu.VMEM)] * len(ins)
        + [pl.BlockSpec(memory_space=pltpu.HBM)] * len(far),
        out_specs=[pl.BlockSpec(memory_space=pltpu.VMEM)] * len(outs),
        out_shape=list(outs),
        scratch_shapes=list(scratch),
        compiler_params=pltpu.CompilerParams(vmem_limit_bytes=room),
        cost_estimate=pl.CostEstimate(flops=flops, bytes_accessed=0, transcendentals=0),
    )(*ins, *far)


def pieces_of(x):
    high = x.astype(bf16)
    wide = high.astype(f32)
    return high, (x - wide).astype(bf16), ((x - wide) + x) * wide


def points_in(x):
    high, low, terms = pieces_of(-2.0 * x.T)
    return high, low, jnp.sum(terms, axis=0, keepdims=True) * 0.25


def crossed(high, low, xh, xl):
    return dot(high, xh) + dot(low, xh) + dot(high, xl)


def entries(cross, square, xsq):
    dist = jnp.maximum(cross + (square + xsq), 0.0) + softening
    return jnp.exp(dist * lax.rsqrt(dist) * (-1.0 / kernel_scale))


def staged(count, cross, finish):
    held = cross(0)
    for i in range(count):
        coming = cross(i + 1) if i + 1 < count else None
        finish(i, held)
        held = coming


def rows_in(x, where, high_ref, low_ref, square_ref):
    high, low, terms = pieces_of(x)
    high_ref[where, :] = high
    low_ref[where, :] = low
    square_ref[where, :] = jnp.sum(terms, axis=1, keepdims=True)
    return high, low


def own_block(ref, share):
    at = lax.rem(place()[0], ref.shape[0] // share) * share
    return ref[pl.ds(pl.multiple_of(at, share), share), :]


def load_kernel(c_hbm, ch_ref, cl_ref, sq_ref, first_ref, shift_ref, c_ref, sems):
    loads = sems.shape[0]
    load = c_ref.shape[0] // loads
    copies = [
        pltpu.make_async_copy(c_hbm.at[pl.ds(i * load, load)], c_ref.at[pl.ds(i * load, load)], sems.at[i])
        for i in range(loads)
    ]
    for copy in copies:
        copy.start()
    for i, copy in enumerate(copies):
        copy.wait()
        where = slice(i * load, (i + 1) * load)
        if i == 0:
            shift_ref[...] = jnp.sum(c_ref[where, :], axis=0, keepdims=True) * (1.0 / load)
        rows_in(c_ref[where, :] - shift_ref[...], where, ch_ref, cl_ref, sq_ref)
    first_ref[...] = own_block(c_ref, first_ref.shape[0])


def first_data_kernel(block, x_ref, shift_ref, ch_ref, cl_ref, sq_ref, c_hbm, *refs):
    kh_ref, kl_ref, xh_ref, xl_ref, xsq_ref, rest_ref, sem = refs
    half = rest_ref.shape[0]
    copy = pltpu.make_async_copy(c_hbm.at[pl.ds(half, half)], rest_ref, sem)
    copy.start()
    xh, xl, xsq = points_in(x_ref[...] - shift_ref[...])
    xh_ref[...] = xh
    xl_ref[...] = xl
    xsq_ref[...] = xsq

    def cross(i):
        where = slice(i * block, (i + 1) * block)
        return crossed(ch_ref[where, :], cl_ref[where, :], xh_ref[...], xl_ref[...])

    def finish(i, value):
        where = slice(i * block, (i + 1) * block)
        kh, kl = split(entries(value, sq_ref[where, :], xsq))
        kh_ref[where, :] = kh
        kl_ref[where, :] = kl

    staged(half // block, cross, finish)
    copy.wait()


def second_data_kernel(block, w_ref, rest_ref, pair0_ref, shift_ref, xh_ref, xl_ref, xsq_ref, first_h, first_l, *refs):
    ch_ref, cl_ref, sq_ref, kh_ref, kl_ref, pred_ref, pair_ref = refs
    half, outs, share = rest_ref.shape[0], pred_ref.shape[0], pair0_ref.shape[0]
    pair_ref[:share, :] = pair0_ref[...]
    pair_ref[share:, :] = own_block(rest_ref, share)

    def cross(i):
        where = slice(i * block, (i + 1) * block)
        high, low = rows_in(rest_ref[where, :] - shift_ref[...], where, ch_ref, cl_ref, sq_ref)
        return crossed(high, low, xh_ref[...], xl_ref[...])

    def finish(i, value):
        where = slice(i * block, (i + 1) * block)
        kh, kl = split(entries(value, sq_ref[where, :], xsq_ref[...]))
        kh_ref[where, :] = kh
        kl_ref[where, :] = kl

    staged(half // block, cross, finish)
    weights = jnp.concatenate(split(w_ref[...]), axis=0)
    pred = dot(weights[:, :half], first_h[...]) + dot(weights[:, :half], first_l[...])
    pred = pred + (dot(weights[:, half:], kh_ref[...]) + dot(weights[:, half:], kl_ref[...]))
    pred_ref[...] = pred[:outs, :] + pred[outs:, :]


def centre_kernel(block, *refs):
    x_refs, shift_ref, centres = refs[:-12], refs[-12], (refs[-11:-8], refs[-8:-5])
    kh_ref, kl_ref, sum_ref, xh_ref, xl_ref = refs[-5:]
    half = centres[0][0].shape[0]
    at = 0
    for x_ref in x_refs:
        span = slice(at, at + x_ref.shape[0])
        at = span.stop
        xh, xl, xsq = points_in(x_ref[...] - shift_ref[...])
        xh_ref[...] = xh
        xl_ref[...] = xl
        sums = []

        def cross(i):
            high, low, _ = centres[i * block // half]
            where = slice(i * block % half, i * block % half + block)
            return crossed(high[where, :], low[where, :], xh_ref[...], xl_ref[...])

        def finish(i, value):
            square = centres[i * block // half][2]
            tile = entries(value, square[i * block % half : i * block % half + block, :], xsq)
            where = slice(i * block, (i + 1) * block)
            kh, kl = split(tile)
            kh_ref[where, span] = kh
            kl_ref[where, span] = kl
            sums.append(jnp.sum(tile.reshape(-1, 8, tile.shape[1]), axis=0))

        staged(2 * half // block, cross, finish)
        sum_ref[:, span] = sum(sums[1:], sums[0])


def share_blocks(mids, flip, tops=(0, 1)):
    _, core, mid, _ = place()
    return [(top, 2 * (mid ^ m) + (core ^ flip)) for m in range(mids) for top in tops]


def take(ref, spot, share):
    top, block = spot
    source = ref[top] if isinstance(ref, tuple) else ref
    at = block if isinstance(ref, tuple) else top * (source.shape[0] // share // 2) + block
    return source[pl.ds(pl.multiple_of(at * share, share), share), :]


def back(where, share, parts, left, out_ref):
    outs = left.shape[0] // 2
    for j, spot in enumerate(where):
        product, at = 0.0, 0
        for high, low in parts:
            high, low = take(high, spot, share), take(low, spot, share)
            values = left[:, at : at + high.shape[1]]
            at += high.shape[1]
            product = product + (dot_rows(values, high) + dot_rows(values, low))
        out_ref[:outs, j * share : (j + 1) * share] = product[:outs] + product[outs:]


def grad_kernel(mids, share, *refs):
    t_ref, kernels, (out_ref, res_ref, left_ref) = refs[-8], refs[-7:-3], refs[-3:]
    total = refs[0][...]
    for ref in refs[1:-8]:
        total = total + ref[...]
    residual = total - t_ref[...]
    res_ref[...] = residual
    left = jnp.concatenate(split(residual), axis=0)
    left_ref[...] = left
    back(share_blocks(mids, 1), share, [(kernels[:2], kernels[2:])], left, out_ref)


def grad_keep_kernel(mids, share, left_ref, *refs):
    back(share_blocks(mids, 0), share, [(refs[:2], refs[2:4])], left_ref[...], refs[4])


def image_kernel(mids, share, shards, *refs):
    kernels = refs[shards : shards + 4]
    out_ref, left_ref, own_ref, max_ref, image_ref = refs[shards + 4 :]
    outs, size = own_ref.shape[0], 2 * share
    total = refs[0][...]
    for ref in refs[1:shards]:
        total = total + ref[...]
    largest = jnp.max(total[outs : outs + 1], keepdims=True)
    max_ref[...] = jnp.broadcast_to(largest, max_ref.shape)
    out_ref[outs:, :] = jnp.broadcast_to(largest, (8, out_ref.shape[1]))
    image_ref[...] = total[:outs]
    for j in range(shards):
        part = image_ref[:, pl.ds(shard_at(j, shards, size), size)]
        left_ref[:, j * size : (j + 1) * size] = jnp.concatenate(split(part), axis=0)
        if j == 0:
            own_ref[...] = jnp.where(place()[3] == 1, part[:, share:], part[:, :share])
    where = share_blocks(mids, 1, [place()[3]])
    back(where, share, [kernels[:2], kernels[2:]], left_ref[...], out_ref)


def image_keep_kernel(mids, share, left_ref, *refs):
    where = share_blocks(mids, 0, [place()[3]])
    back(where, share, [refs[:2], refs[2:4]], left_ref[...], refs[-1])


def shard_at(j, shards, share):
    return pl.multiple_of(lax.rem(lax.axis_index("centre") + j, shards) * share, share)


def rows_of(ref, where, share):
    return jnp.concatenate([take(ref, spot, share) for spot in where], axis=0)


def product(mids, share, flip, pieces, kernels):
    where = share_blocks(mids, flip)
    high, low = split(jnp.concatenate([ref[...] for ref in pieces], axis=1))
    left = jnp.concatenate([high, low], axis=0)
    outs = high.shape[0]
    for kh, kl in (kernels[:2], kernels[2:]):
        result = dot(left, rows_of(kh, where, share)) + dot(left, rows_of(kl, where, share))
        yield result[:outs] + result[outs:]


def first_kernel(mids, share, *refs):
    own_ref, far_ref = refs[-2:]
    own, far = product(mids, share, 0, refs[:mids], refs[mids : mids + 4])
    own_ref[...] = own
    far_ref[...] = far


def second_kernel(mids, share, shards, *refs):
    own_ref, far_ref, osum, fsum, out_ref = refs[-5:]
    outs, size = own_ref.shape[0], 2 * share
    own, far = product(mids, share, 1, refs[:-9], refs[-9:-5])
    own, far = own + own_ref[...], far + far_ref[...]
    for j in range(shards):
        source, sums, at = (own, osum, 0) if j == 0 else (far, fsum, size * (j - 1))
        where = pl.ds(shard_at(j, shards, size), size)
        out_ref[:outs, where] = source[:, at : at + size]
        row_sums = jnp.sum(sums[:, at : at + size], axis=0, keepdims=True)
        out_ref[outs:, where] = jnp.broadcast_to(row_sums, (8, size))


def pack_kernel(*refs):
    refs[-1][...] = jnp.concatenate([ref[...] for ref in refs[:-1]], axis=1)


def join_kernel(mids, keep_ref, got_ref, *refs):
    outs = keep_ref.shape[0]
    piece_refs = refs[-mids:]
    wide = piece_refs[0].shape[1]
    for m in range(mids):
        columns = slice(m * wide, (m + 1) * wide)
        piece_refs[m][:outs, :] = keep_ref[:, columns] + got_ref[:outs, columns]
    if len(refs) > mids:
        largest = jnp.maximum(refs[0][...], got_ref[outs:, : refs[0].shape[1]])
        for m in range(mids):
            piece_refs[m][outs:, :] = jnp.broadcast_to(largest[:, :1], (8, wide))


def sum_kernel(*refs):
    total = refs[0][...]
    for ref in refs[1:-1]:
        total = total + ref[...]
    refs[-1][...] = total


def final_kernel(mids, whole_ref, own_ref, coeff_ref, *refs):
    pieces, out_ref = refs[:mids], refs[mids]
    outs, share = out_ref.shape
    second = pieces[0][:outs, :]
    largest = pieces[0][outs:, :]
    for ref in pieces[1:]:
        second = second + ref[:outs, :]
        largest = jnp.maximum(largest, ref[outs:, :])
    step = 1.0 / largest[:1, :1]
    index, _, _, top = place()
    gradient = jnp.where(top == 1, whole_ref[:, share:], whole_ref[:, :share])
    theta = 3.0 * step * (gradient - step * own_ref[...]) + (step * step * step) * second
    coefficients = coeff_ref[:, pl.ds(pl.multiple_of(index * share, share), share)]
    out_ref[...] = coefficients - learning_rate * theta


def send_xor(array, mask):
    count = lax.axis_size("dp")
    return lax.ppermute(array, "dp", [(i, i ^ mask) for i in range(count)])


def send_far(array, mask, shift):
    dp, centre = lax.axis_size("dp"), lax.axis_size("centre")
    pairs = [
        (d * centre + c, (d ^ mask) * centre + (c + shift) % centre)
        for d in range(dp)
        for c in range(centre)
    ]
    return lax.ppermute(array, ("dp", "centre"), pairs)


def after(value, *others):
    return lax.optimization_barrier((value, *others))[0]


def body(samples, targets, centres, coefficients):
    count = lax.axis_size("dp")
    shards = lax.axis_size("centre")
    rows, width = centres.shape
    share = rows // count
    points, outs = targets.shape
    half = count // 2
    mids = half // 2
    weights = coefficients.T
    block = min(256, rows)

    part = rows // 2
    loads = min(4, count)
    kept = 4 * part * width + 512 * part + 4 * share * width
    *loaded, first, shift = call(
        load_kernel, "load", [],
        [
            like(part, width, dtype=bf16),
            like(part, width, dtype=bf16),
            like(part, 1),
            like(share, width),
            like(1, width),
        ],
        [pltpu.VMEM((part, width), f32), pltpu.SemaphoreType.DMA((loads,))],
        room=53 * mega - kept - 4 * points * width, far=[centres],
    )
    kept = 2 * kept + 8 * points * width + 4 * part * (points + width)
    kh0, kl0, xh, xl, xsq, rest = call(
        functools.partial(first_data_kernel, block // 2), "data_first", [samples, shift] + loaded,
        [
            like(part, points, dtype=bf16),
            like(part, points, dtype=bf16),
            like(width, points, dtype=bf16),
            like(width, points, dtype=bf16),
            like(1, points),
            like(part, width),
        ],
        [pltpu.SemaphoreType.DMA],
        room=107 * mega // 2 - kept, far=[centres],
    )
    ch, cl, square, kh1, kl1, pred, pair = call(
        functools.partial(second_data_kernel, block // 2), "data_second",
        [weights, rest, first, shift, xh, xl, xsq, kh0, kl0],
        [
            like(part, width, dtype=bf16),
            like(part, width, dtype=bf16),
            like(part, 1),
            like(part, points, dtype=bf16),
            like(part, points, dtype=bf16),
            like(outs, points),
            like(2 * share, width),
        ],
    )
    halves = loaded + [ch, cl, square]
    kernel = [kh0, kh1, kl0, kl1]
    got = [send_far(pred, 0, shift) for shift in range(1, shards)]
    far = [send_far(pair, 0, -shift) for shift in range(1, shards)]

    def centre_tile(blocks, name):
        size = blocks[0].shape[0]
        columns = size * len(blocks)
        return call(
            functools.partial(centre_kernel, block // 2), name, blocks + [shift] + halves,
            [like(rows, columns, dtype=bf16), like(rows, columns, dtype=bf16), like(8, columns)],
            [pltpu.VMEM((width, size), bf16), pltpu.VMEM((width, size), bf16)],
            flops=6 * rows * columns * width,
        )

    own_high, own_low, own_sums = centre_tile([after(pair, pred)], "own_tile")
    got[0] = after(got[0], own_high)

    give, residual, left = call(
        functools.partial(grad_kernel, mids, share), "grad_give",
        [pred] + got + [targets.T] + kernel,
        [like(outs, half * share), like(outs, points), like(2 * outs, points, dtype=bf16)],
    )
    received = send_xor(give, 1)
    (keep,) = call(
        functools.partial(grad_keep_kernel, mids, share), "grad_keep",
        [left] + kernel, [like(outs, half * share)],
    )

    def join(keep, received, extra, height):
        return call(
            functools.partial(join_kernel, mids), "join",
            [keep, received] + extra, [like(height, keep.shape[1] // mids)] * mids,
        )

    def total(arrays):
        return call(sum_kernel, "sum", arrays, [like(*arrays[0].shape)])[0]

    def spread(pieces):
        sent = [send_xor(pieces[m], 2 * m) for m in range(mids - 1, 0, -1)]
        return [pieces[0]] + sent[::-1]

    part = total(spread(join(keep, received, [], outs)))
    whole = total([part, send_xor(part, half)])
    gathered = spread([whole] * mids)
    far_high, far_low, far_sums = centre_tile([after(f, whole) for f in far], "far_tile")
    kernels = [own_high, own_low, far_high, far_low]
    wide = 2 * share * (shards - 1)
    packed = call(
        pack_kernel, "pack", [after(whole, far_sums)] + gathered[1:], [like(outs, 2 * share * mids)]
    )[0]
    swapped = [send_xor(packed, 1)]
    firsts = call(
        functools.partial(first_kernel, mids, share), "product_first",
        gathered + kernels, [like(outs, 2 * share), like(outs, wide)],
    )
    (image,) = call(
        functools.partial(second_kernel, mids, share, shards), "product_second",
        swapped + kernels + list(firsts) + [own_sums, far_sums],
        [like(outs + 8, 2 * share * shards)],
    )
    images = [image] + [send_far(image, 0, shift) for shift in range(1, shards)]
    give, left, own, largest = call(
        functools.partial(image_kernel, mids, share, shards), "image_give",
        images + kernels,
        [
            like(outs + 8, mids * share),
            like(2 * outs, 2 * share * shards, dtype=bf16),
            like(outs, share),
            like(8, share),
        ],
        [pltpu.VMEM((outs, 2 * share * shards), f32)],
    )
    received = send_xor(give, 1)
    (keep,) = call(
        functools.partial(image_keep_kernel, mids, share), "image_keep",
        [left] + kernels, [like(outs, mids * share)],
    )
    pieces = spread(join(keep, received, [largest], outs + 8))
    (new_coefficients,) = call(
        functools.partial(final_kernel, mids), "final", [whole, own, weights] + pieces, [like(outs, share)]
    )
    return (residual.T, new_coefficients.T)


def solution(mesh):
    return jax.shard_map(
        body,
        mesh=mesh,
        in_specs=(P("dp", None), P("dp", None), P("centre", None), P("centre", None)),
        out_specs=(P("dp", None), P(("centre", "dp"), None)),
        check_vma=False,
    )
```

```python
import functools
import jax
import jax.numpy as jnp
from jax import lax
from jax.experimental import pallas as pl
from jax.experimental.pallas import tpu as pltpu
from jax.sharding import PartitionSpec as P

softening = 0.01
kernel_scale = 0.2
learning_rate = 4.0
f32, bf16 = jnp.float32, jnp.bfloat16
mega = 1024 * 1024


def split(x):
    high = x.astype(bf16)
    return high, (x - high.astype(f32)).astype(bf16)


def dot(left, right):
    return jnp.dot(left, right, preferred_element_type=f32)


def dot_rows(left, right):
    return lax.dot_general(left, right, (((1,), (1,)), ((), ())), preferred_element_type=f32)


def place():
    index, count = lax.axis_index("dp"), lax.axis_size("dp")
    return index, lax.rem(index, 2), lax.rem(index // 2, count // 4), index // (count // 2)


def like(*shape, dtype=f32):
    return jax.ShapeDtypeStruct(shape, dtype)


def call(kernel, name, ins, outs, scratch=(), room=8 * mega, flops=0, far=()):
    return pl.pallas_call(
        kernel,
        name=name,
        in_specs=[pl.BlockSpec(memory_space=pltpu.VMEM)] * len(ins)
        + [pl.BlockSpec(memory_space=pltpu.HBM)] * len(far),
        out_specs=[pl.BlockSpec(memory_space=pltpu.VMEM)] * len(outs),
        out_shape=list(outs),
        scratch_shapes=list(scratch),
        compiler_params=pltpu.CompilerParams(vmem_limit_bytes=room),
        cost_estimate=pl.CostEstimate(flops=flops, bytes_accessed=0, transcendentals=0),
    )(*ins, *far)


def pieces_of(x):
    high = x.astype(bf16)
    wide = high.astype(f32)
    return high, (x - wide).astype(bf16), ((x - wide) + x) * wide


def points_in(x):
    high, low, terms = pieces_of(-2.0 * x.T)
    return high, low, jnp.sum(terms, axis=0, keepdims=True) * 0.25


def crossed(high, low, xh, xl):
    return dot(high, xh) + dot(low, xh) + dot(high, xl)


def entries(cross, square, xsq):
    dist = jnp.maximum(cross + (square + xsq), 0.0) + softening
    return jnp.exp(dist * lax.rsqrt(dist) * (-1.0 / kernel_scale))


def staged(count, cross, finish):
    held = cross(0)
    for i in range(count):
        coming = cross(i + 1) if i + 1 < count else None
        finish(i, held)
        held = coming


def rows_in(x, where, high_ref, low_ref, square_ref):
    high, low, terms = pieces_of(x)
    high_ref[where, :] = high
    low_ref[where, :] = low
    square_ref[where, :] = jnp.sum(terms, axis=1, keepdims=True)
    return high, low


def own_block(ref, share):
    at = lax.rem(place()[0], ref.shape[0] // share) * share
    return ref[pl.ds(pl.multiple_of(at, share), share), :]


def load_kernel(c_hbm, ch_ref, cl_ref, sq_ref, first_ref, shift_ref, c_ref, sems):
    loads = sems.shape[0]
    load = c_ref.shape[0] // loads
    copies = [
        pltpu.make_async_copy(c_hbm.at[pl.ds(i * load, load)], c_ref.at[pl.ds(i * load, load)], sems.at[i])
        for i in range(loads)
    ]
    for copy in copies:
        copy.start()
    for i, copy in enumerate(copies):
        copy.wait()
        where = slice(i * load, (i + 1) * load)
        if i == 0:
            shift_ref[...] = jnp.sum(c_ref[where, :], axis=0, keepdims=True) * (1.0 / load)
        rows_in(c_ref[where, :] - shift_ref[...], where, ch_ref, cl_ref, sq_ref)
    first_ref[...] = own_block(c_ref, first_ref.shape[0])


def first_data_kernel(block, x_ref, shift_ref, ch_ref, cl_ref, sq_ref, c_hbm, *refs):
    kh_ref, kl_ref, xh_ref, xl_ref, xsq_ref, rest_ref, sem = refs
    half = rest_ref.shape[0]
    copy = pltpu.make_async_copy(c_hbm.at[pl.ds(half, half)], rest_ref, sem)
    copy.start()
    xh, xl, xsq = points_in(x_ref[...] - shift_ref[...])
    xh_ref[...] = xh
    xl_ref[...] = xl
    xsq_ref[...] = xsq

    def cross(i):
        where = slice(i * block, (i + 1) * block)
        return crossed(ch_ref[where, :], cl_ref[where, :], xh_ref[...], xl_ref[...])

    def finish(i, value):
        where = slice(i * block, (i + 1) * block)
        kh, kl = split(entries(value, sq_ref[where, :], xsq))
        kh_ref[where, :] = kh
        kl_ref[where, :] = kl

    staged(half // block, cross, finish)
    copy.wait()


def second_data_kernel(block, w_ref, rest_ref, pair0_ref, shift_ref, xh_ref, xl_ref, xsq_ref, first_h, first_l, *refs):
    ch_ref, cl_ref, sq_ref, kh_ref, kl_ref, pred_ref, pair_ref = refs
    half, outs, share = rest_ref.shape[0], pred_ref.shape[0], pair0_ref.shape[0]
    pair_ref[:share, :] = pair0_ref[...]
    pair_ref[share:, :] = own_block(rest_ref, share)

    def cross(i):
        where = slice(i * block, (i + 1) * block)
        high, low = rows_in(rest_ref[where, :] - shift_ref[...], where, ch_ref, cl_ref, sq_ref)
        return crossed(high, low, xh_ref[...], xl_ref[...])

    def finish(i, value):
        where = slice(i * block, (i + 1) * block)
        kh, kl = split(entries(value, sq_ref[where, :], xsq_ref[...]))
        kh_ref[where, :] = kh
        kl_ref[where, :] = kl

    staged(half // block, cross, finish)
    weights = jnp.concatenate(split(w_ref[...]), axis=0)
    pred = dot(weights[:, :half], first_h[...]) + dot(weights[:, :half], first_l[...])
    pred = pred + (dot(weights[:, half:], kh_ref[...]) + dot(weights[:, half:], kl_ref[...]))
    pred_ref[...] = pred[:outs, :] + pred[outs:, :]


def centre_kernel(block, *refs):
    x_refs, shift_ref, centres = refs[:-12], refs[-12], (refs[-11:-8], refs[-8:-5])
    kh_ref, kl_ref, sum_ref, xh_ref, xl_ref = refs[-5:]
    half = centres[0][0].shape[0]
    at = 0
    for x_ref in x_refs:
        span = slice(at, at + x_ref.shape[0])
        at = span.stop
        xh, xl, xsq = points_in(x_ref[...] - shift_ref[...])
        xh_ref[...] = xh
        xl_ref[...] = xl
        sums = []

        def cross(i):
            high, low, _ = centres[i * block // half]
            where = slice(i * block % half, i * block % half + block)
            return crossed(high[where, :], low[where, :], xh_ref[...], xl_ref[...])

        def finish(i, value):
            square = centres[i * block // half][2]
            tile = entries(value, square[i * block % half : i * block % half + block, :], xsq)
            where = slice(i * block, (i + 1) * block)
            kh, kl = split(tile)
            kh_ref[where, span] = kh
            kl_ref[where, span] = kl
            sums.append(jnp.sum(tile.reshape(-1, 8, tile.shape[1]), axis=0))

        staged(2 * half // block, cross, finish)
        sum_ref[:, span] = sum(sums[1:], sums[0])


def share_blocks(mids, flip, tops=(0, 1)):
    _, core, mid, _ = place()
    return [(top, 2 * (mid ^ m) + (core ^ flip)) for m in range(mids) for top in tops]


def take(ref, spot, share):
    top, block = spot
    source = ref[top] if isinstance(ref, tuple) else ref
    at = block if isinstance(ref, tuple) else top * (source.shape[0] // share // 2) + block
    return source[pl.ds(pl.multiple_of(at * share, share), share), :]


def back(where, share, parts, left, out_ref):
    outs = left.shape[0] // 2
    for j, spot in enumerate(where):
        product, at = 0.0, 0
        for high, low in parts:
            high, low = take(high, spot, share), take(low, spot, share)
            values = left[:, at : at + high.shape[1]]
            at += high.shape[1]
            product = product + (dot_rows(values, high) + dot_rows(values, low))
        out_ref[:outs, j * share : (j + 1) * share] = product[:outs] + product[outs:]


def grad_kernel(mids, share, *refs):
    t_ref, kernels, (out_ref, res_ref, left_ref) = refs[-8], refs[-7:-3], refs[-3:]
    total = refs[0][...]
    for ref in refs[1:-8]:
        total = total + ref[...]
    residual = total - t_ref[...]
    res_ref[...] = residual
    left = jnp.concatenate(split(residual), axis=0)
    left_ref[...] = left
    back(share_blocks(mids, 1), share, [(kernels[:2], kernels[2:])], left, out_ref)


def grad_keep_kernel(mids, share, left_ref, *refs):
    back(share_blocks(mids, 0), share, [(refs[:2], refs[2:4])], left_ref[...], refs[4])


def image_kernel(mids, share, shards, *refs):
    sums, kernels = refs[shards : 2 * shards], refs[2 * shards : 2 * shards + 4]
    out_ref, left_ref, own_ref, max_ref, image_ref = refs[2 * shards + 4 :]
    outs, size = own_ref.shape[0], 2 * share
    total = refs[0][...]
    for ref in refs[1:shards]:
        total = total + ref[...]
    row_sums = sums[0][...]
    for ref in sums[1:]:
        row_sums = row_sums + ref[...]
    largest = jnp.max(row_sums[:1], keepdims=True)
    max_ref[...] = jnp.broadcast_to(largest, max_ref.shape)
    out_ref[outs:, :] = jnp.broadcast_to(largest, (8, out_ref.shape[1]))
    image_ref[...] = total
    for j in range(shards):
        part = image_ref[:, pl.ds(shard_at(j, shards, size), size)]
        left_ref[:, j * size : (j + 1) * size] = jnp.concatenate(split(part), axis=0)
        if j == 0:
            own_ref[...] = jnp.where(place()[3] == 1, part[:, share:], part[:, :share])
    where = share_blocks(mids, 1, [place()[3]])
    back(where, share, [kernels[:2], kernels[2:]], left_ref[...], out_ref)


def image_keep_kernel(mids, share, left_ref, *refs):
    where = share_blocks(mids, 0, [place()[3]])
    back(where, share, [refs[:2], refs[2:4]], left_ref[...], refs[-1])


def shard_at(j, shards, share):
    return pl.multiple_of(lax.rem(lax.axis_index("centre") + j, shards) * share, share)


def rows_of(ref, where, share):
    return jnp.concatenate([take(ref, spot, share) for spot in where], axis=0)


def product(mids, share, flip, pieces, kernels):
    where = share_blocks(mids, flip)
    high, low = split(jnp.concatenate([ref[...] for ref in pieces], axis=1))
    left = jnp.concatenate([high, low], axis=0)
    outs = high.shape[0]
    for kh, kl in (kernels[:2], kernels[2:]):
        result = dot(left, rows_of(kh, where, share)) + dot(left, rows_of(kl, where, share))
        yield result[:outs] + result[outs:]


def first_kernel(mids, share, *refs):
    own_ref, far_ref = refs[-2:]
    own, far = product(mids, share, 0, refs[:mids], refs[mids : mids + 4])
    own_ref[...] = own
    far_ref[...] = far


def second_kernel(mids, share, shards, *refs):
    own_ref, far_ref, out_ref = refs[-3:]
    size = 2 * share
    own, far = product(mids, share, 1, refs[:-7], refs[-7:-3])
    own, far = own + own_ref[...], far + far_ref[...]
    for j in range(shards):
        source, at = (own, 0) if j == 0 else (far, size * (j - 1))
        out_ref[:, pl.ds(shard_at(j, shards, size), size)] = source[:, at : at + size]


def row_sums_kernel(shards, size, own_ref, far_ref, out_ref):
    for j in range(shards):
        source, at = (own_ref, 0) if j == 0 else (far_ref, size * (j - 1))
        sums = jnp.sum(source[:, at : at + size], axis=0, keepdims=True)
        out_ref[:, pl.ds(shard_at(j, shards, size), size)] = jnp.broadcast_to(sums, (8, size))


def join_kernel(mids, keep_ref, got_ref, *refs):
    outs = keep_ref.shape[0]
    piece_refs = refs[-mids:]
    wide = piece_refs[0].shape[1]
    for m in range(mids):
        columns = slice(m * wide, (m + 1) * wide)
        piece_refs[m][:outs, :] = keep_ref[:, columns] + got_ref[:outs, columns]
    if len(refs) > mids:
        largest = jnp.maximum(refs[0][...], got_ref[outs:, : refs[0].shape[1]])
        for m in range(mids):
            piece_refs[m][outs:, :] = jnp.broadcast_to(largest[:, :1], (8, wide))


def sum_kernel(*refs):
    total = refs[0][...]
    for ref in refs[1:-1]:
        total = total + ref[...]
    refs[-1][...] = total


def final_kernel(mids, whole_ref, own_ref, coeff_ref, *refs):
    pieces, out_ref = refs[:mids], refs[mids]
    outs, share = out_ref.shape
    second = pieces[0][:outs, :]
    largest = pieces[0][outs:, :]
    for ref in pieces[1:]:
        second = second + ref[:outs, :]
        largest = jnp.maximum(largest, ref[outs:, :])
    step = 1.0 / largest[:1, :1]
    index, _, _, top = place()
    gradient = jnp.where(top == 1, whole_ref[:, share:], whole_ref[:, :share])
    theta = 3.0 * step * (gradient - step * own_ref[...]) + (step * step * step) * second
    coefficients = coeff_ref[:, pl.ds(pl.multiple_of(index * share, share), share)]
    out_ref[...] = coefficients - learning_rate * theta


def send_xor(array, mask):
    count = lax.axis_size("dp")
    return lax.ppermute(array, "dp", [(i, i ^ mask) for i in range(count)])


def send_far(array, mask, shift):
    dp, centre = lax.axis_size("dp"), lax.axis_size("centre")
    pairs = [
        (d * centre + c, (d ^ mask) * centre + (c + shift) % centre)
        for d in range(dp)
        for c in range(centre)
    ]
    return lax.ppermute(array, ("dp", "centre"), pairs)


def after(value, *others):
    return lax.optimization_barrier((value, *others))[0]


def body(samples, targets, centres, coefficients):
    count = lax.axis_size("dp")
    shards = lax.axis_size("centre")
    rows, width = centres.shape
    share = rows // count
    points, outs = targets.shape
    half = count // 2
    mids = half // 2
    weights = coefficients.T
    block = min(256, rows)

    part = rows // 2
    loads = min(4, count)
    kept = 4 * part * width + 512 * part + 4 * share * width
    *loaded, first, shift = call(
        load_kernel, "load", [],
        [
            like(part, width, dtype=bf16),
            like(part, width, dtype=bf16),
            like(part, 1),
            like(share, width),
            like(1, width),
        ],
        [pltpu.VMEM((part, width), f32), pltpu.SemaphoreType.DMA((loads,))],
        room=53 * mega - kept - 4 * points * width, far=[centres],
    )
    kept = 2 * kept + 8 * points * width + 4 * part * (points + width)
    kh0, kl0, xh, xl, xsq, rest = call(
        functools.partial(first_data_kernel, block // 2), "data_first", [samples, shift] + loaded,
        [
            like(part, points, dtype=bf16),
            like(part, points, dtype=bf16),
            like(width, points, dtype=bf16),
            like(width, points, dtype=bf16),
            like(1, points),
            like(part, width),
        ],
        [pltpu.SemaphoreType.DMA],
        room=107 * mega // 2 - kept, far=[centres],
    )
    ch, cl, square, kh1, kl1, pred, pair = call(
        functools.partial(second_data_kernel, block // 2), "data_second",
        [weights, rest, first, shift, xh, xl, xsq, kh0, kl0],
        [
            like(part, width, dtype=bf16),
            like(part, width, dtype=bf16),
            like(part, 1),
            like(part, points, dtype=bf16),
            like(part, points, dtype=bf16),
            like(outs, points),
            like(2 * share, width),
        ],
    )
    halves = loaded + [ch, cl, square]
    kernel = [kh0, kh1, kl0, kl1]
    got = [send_far(pred, 0, shift) for shift in range(1, shards)]
    far = [send_far(pair, 0, -shift) for shift in range(1, shards)]

    def centre_tile(blocks, name):
        size = blocks[0].shape[0]
        columns = size * len(blocks)
        return call(
            functools.partial(centre_kernel, block // 2), name, blocks + [shift] + halves,
            [like(rows, columns, dtype=bf16), like(rows, columns, dtype=bf16), like(8, columns)],
            [pltpu.VMEM((width, size), bf16), pltpu.VMEM((width, size), bf16)],
            flops=6 * rows * columns * width,
        )

    own_high, own_low, own_sums = centre_tile([after(pair, pred)], "own_tile")
    got[0] = after(got[0], own_high)

    give, residual, left = call(
        functools.partial(grad_kernel, mids, share), "grad_give",
        [pred] + got + [targets.T] + kernel,
        [like(outs, half * share), like(outs, points), like(2 * outs, points, dtype=bf16)],
    )
    received = send_xor(give, 1)
    (keep,) = call(
        functools.partial(grad_keep_kernel, mids, share), "grad_keep",
        [left] + kernel, [like(outs, half * share)],
    )

    def join(keep, received, extra, height):
        return call(
            functools.partial(join_kernel, mids), "join",
            [keep, received] + extra, [like(height, keep.shape[1] // mids)] * mids,
        )

    def total(arrays):
        return call(sum_kernel, "sum", arrays, [like(*arrays[0].shape)])[0]

    def spread(pieces):
        sent = [send_xor(pieces[m], 2 * m) for m in range(mids - 1, 0, -1)]
        return [pieces[0]] + sent[::-1]

    part = total(spread(join(keep, received, [], outs)))
    whole = total([part, send_xor(part, half)])
    gathered = spread([whole] * mids)
    far_high, far_low, far_sums = centre_tile([after(f, whole) for f in far], "far_tile")
    kernels = [own_high, own_low, far_high, far_low]
    wide = 2 * share * (shards - 1)
    (sums,) = call(
        functools.partial(row_sums_kernel, shards, 2 * share), "row_sums",
        [own_sums, far_sums], [like(8, 2 * share * shards)],
    )
    sums = [sums] + [send_far(sums, 0, shift) for shift in range(1, shards)]
    swapped = [send_xor(whole, 1)] + [send_xor(after(piece, far_sums), 1) for piece in gathered[1:]]
    firsts = call(
        functools.partial(first_kernel, mids, share), "product_first",
        gathered + kernels, [like(outs, 2 * share), like(outs, wide)],
    )
    (image,) = call(
        functools.partial(second_kernel, mids, share, shards), "product_second",
        swapped + kernels + list(firsts), [like(outs, 2 * share * shards)],
    )
    images = [image] + [send_far(image, 0, shift) for shift in range(1, shards)]
    give, left, own, largest = call(
        functools.partial(image_kernel, mids, share, shards), "image_give",
        images + sums + kernels,
        [
            like(outs + 8, mids * share),
            like(2 * outs, 2 * share * shards, dtype=bf16),
            like(outs, share),
            like(8, share),
        ],
        [pltpu.VMEM((outs, 2 * share * shards), f32)],
    )
    received = send_xor(give, 1)
    (keep,) = call(
        functools.partial(image_keep_kernel, mids, share), "image_keep",
        [left] + kernels, [like(outs, mids * share)],
    )
    pieces = spread(join(keep, received, [largest], outs + 8))
    (new_coefficients,) = call(
        functools.partial(final_kernel, mids), "final", [whole, own, weights] + pieces, [like(outs, share)]
    )
    return (residual.T, new_coefficients.T)


def solution(mesh):
    return jax.shard_map(
        body,
        mesh=mesh,
        in_specs=(P("dp", None), P("dp", None), P("centre", None), P("centre", None)),
        out_specs=(P("dp", None), P(("centre", "dp"), None)),
        check_vma=False,
    )
```
